256 devices in a mesh: node: 16 (over z_lo, y), local: 16 (over x, z_hi, core).
Axes of the slice: x: 4, y: 4, z: 8 (z_hi: 2, z_lo: 4; z = z_hi * 4 + z_lo), core: 2. Of those that a mesh axis runs over, the one named last changes fastest.
Arguments:
- activations: bfloat16 [65536, 5120], P(('node', 'local')), may hold values from -6 to 6
- queries: bfloat16 [65536, 5120], P(('node', 'local')), may hold values from -100 to 100
- rotated_key_value: bfloat16 [65536, 2048], P(('node', 'local')), may hold values from -5 to 5
- attention_out_grad: bfloat16 [65536, 5120], P(('node', 'local')), may hold values from -6 to 6
- adapter_down: bfloat16 [5120, 128], replicated, may hold values from -0.078125 to 0.078125
- adapter_up: bfloat16 [128, 1024], replicated, may hold values from -0.75 to 0.75
- bin_local_index: int32 [256, 256], P(('node', 'local')), may hold values from 0 to 15, as said below
- bin_row_offset: int32 [256, 256], P(('node', 'local')), may hold values from 0 to 3, as said below
- spill_node: int32 [256, 256], P(('node', 'local')), may hold values from 0 to 15, as said below
- spill_row_offset: int32 [256, 256], P(('node', 'local')), may hold values from 0 to 3, as said below
- arrival_pick_index: int32 [256, 256], P(('node', 'local')), may hold values from 0 to 383, as said below
- packed_sequence_number: int32 [256, 256], P(('node', 'local')), may hold values from 0 to 7, never falling along the last dimension, each value on 1 to 128 neighbouring positions
Outputs:
- key_value_cotangent: bfloat16 [65536, 2048], P(('node', 'local'))
- down_factor_grad: float32 [5120, 128], P(('node', 'local'))
- up_factor_grad_transposed: float32 [1024, 128], P(('node', 'local'))
The draws below stay inside these ranges and needn't reach their ends.
Inputs may be any that keep to these rules, and one draw needn't show every extreme that they name: `bin_local_index`: rows that stay or overflow carry the device's own local index. At most 4 rows of a device go to one other bin of its node, and that bin sends back exactly as many to it; in every node one device sends 4 rows to every other bin of the node. `bin_row_offset`: offsets of the rows one device sends to one bin are 0 up to their count minus 1; zero for other rows. `spill_node`: A row moves across nodes only if it stays in its node's bin of its own local index otherwise; at most 4 rows of a device go to one other node, and as many come back; for every local index one node sends 4 rows to every other node. Rows that do not overflow carry their own node. `spill_row_offset`: offsets of the overflow rows one device sends to one node are 0 up to their count minus 1; zero for other rows. `arrival_pick_index`: every bin holds exactly 256 rows: each row of the arrival list of 384 entries that is filled is named once, and no empty entry is named.
All inputs are finite; a program needn't handle non-finite values.
Results may differ from the reference program's by a relative error of at most 0.0056.
Values may be sent and summed in bfloat16 or wider, within the bound.
No kernel may reach another device: no remote copies, remote signals or barrier semaphores. Data moves between devices by JAX's collectives and lax.ppermute only.
A program may use at most 128 MiB of HBM per device.

```python
import math
import jax
import jax.numpy as jnp
import numpy as np
from jax import lax

MODEL_WIDTH = 5120
KV_HEADS = 8
HEAD = 128
ADAPTER_RANK = 64
TOK_DEV = 256
CAP_L = 4
CAP_N = 4
GROUP = 5
QW = 5120
KEY_HEAD_WIDTH = 1024
BINS = 256
TOKENS = 65536
N_NODE = 16
N_LOCAL = 16


def symmetric_counts(seed_key, groups, members, capacity):
    raw_counts = jax.random.randint(jax.random.fold_in(seed_key, 1), (groups, members, members), 0, capacity + 1)
    upper_half = jnp.triu(raw_counts, 1)
    count_table = upper_half + jnp.swapaxes(upper_half, 1, 2)
    full_row = jax.random.randint(jax.random.fold_in(seed_key, 2), (groups, 1, 1), 0, members)
    member_ids = jnp.arange(members)
    hit_mask = (member_ids[None, :, None] == full_row) | (member_ids[None, None, :] == full_row)
    count_table = jnp.where(hit_mask, capacity, count_table)
    return jnp.where(member_ids[:, None] == member_ids[None, :], 0, count_table)


def route_plan(seed_key):
    within = symmetric_counts(jax.random.fold_in(seed_key, 11), N_NODE, N_LOCAL, CAP_L)
    across = symmetric_counts(jax.random.fold_in(seed_key, 12), N_LOCAL, N_NODE, CAP_N)
    device = jnp.arange(BINS)
    dev_node = device // N_LOCAL
    dev_local = device % N_LOCAL
    send_in = within[dev_node, dev_local]
    send_out = across[dev_local, dev_node]
    recv_in = within[dev_node, :, dev_local]
    recv_out = across[dev_local, :, dev_node]
    cum_in = jnp.cumsum(send_in, axis=1)
    cum_out = jnp.cumsum(send_out, axis=1)
    total_in = cum_in[:, -1:]
    total_out = cum_out[:, -1:]
    ticket = jnp.arange(TOK_DEV)[None, :]
    dest_in = jnp.minimum(jnp.sum(cum_in[:, None, :] <= ticket[:, :, None], axis=2), N_LOCAL - 1)
    off_in = ticket - jnp.take_along_axis(cum_in - send_in, dest_in, axis=1)
    later = ticket - total_in
    dest_out = jnp.minimum(jnp.sum(cum_out[:, None, :] <= later[:, :, None], axis=2), N_NODE - 1)
    off_out = later - jnp.take_along_axis(cum_out - send_out, dest_out, axis=1)
    is_in = ticket < total_in
    is_out = (later >= 0) & (later < total_out)
    perms = jax.vmap(lambda row_key: jax.random.permutation(row_key, TOK_DEV))(jax.random.split(jax.random.fold_in(seed_key, 13), BINS))
    of_row = jnp.argsort(perms, axis=1)

    def by_row(values):
        return jnp.take_along_axis(jnp.broadcast_to(values, (BINS, TOK_DEV)), of_row, axis=1)
    row_in = by_row(is_in)
    row_out = by_row(is_out)
    bin_local_index = jnp.where(row_in, by_row(dest_in), dev_local[:, None])
    bin_row_offset = jnp.where(row_in, by_row(off_in), 0)
    spill_node = jnp.where(row_out, by_row(dest_out), dev_node[:, None])
    spill_row_offset = jnp.where(row_out, by_row(off_out), 0)
    stays = jnp.logical_not(row_in | row_out)
    near_valid = (jnp.arange(CAP_L)[None, None, :] < recv_in[:, :, None]).reshape(BINS, N_LOCAL * CAP_L)
    far_valid = (jnp.arange(CAP_N)[None, None, :] < recv_out[:, :, None]).reshape(BINS, N_NODE * CAP_N)
    valid = jnp.concatenate([stays, near_valid, far_valid], axis=1)
    valid_order = jnp.argsort(jnp.where(valid, 0, 1), axis=1, stable=True)[:, :TOK_DEV]
    shuffle = jax.vmap(lambda row_key: jax.random.permutation(row_key, TOK_DEV))(jax.random.split(jax.random.fold_in(seed_key, 14), BINS))
    arrival_pick_index = jnp.take_along_axis(valid_order, shuffle, axis=1)
    return (bin_local_index.astype(jnp.int32), bin_row_offset.astype(jnp.int32), spill_node.astype(jnp.int32), spill_row_offset.astype(jnp.int32), arrival_pick_index.astype(jnp.int32))


def draw_bin_local_index(key, part):
    return route_plan(key)[0]


def draw_bin_row_offset(key, part):
    return route_plan(key)[1]


def draw_spill_node(key, part):
    return route_plan(key)[2]


def draw_spill_row_offset(key, part):
    return route_plan(key)[3]


def draw_arrival_pick_index(key, part):
    return route_plan(key)[4]


def shared_keys(seed_key):
    return jax.random.truncated_normal(jax.random.fold_in(seed_key, 101), -5.0, 5.0, (TOKENS, KEY_HEAD_WIDTH), jnp.float32)


def draw_queries(key, part):
    key = jax.random.fold_in(key, 3)
    result = jax.random.truncated_normal(jax.random.fold_in(key, 1), -5.0, 5.0, (TOKENS, QW), jnp.float32)
    return result.astype(jnp.bfloat16)


def draw_rotated_key_value(key, part):
    key_rows = shared_keys(key)
    key = jax.random.fold_in(key, 5)
    value_rows = jax.random.truncated_normal(jax.random.fold_in(key, 1), -5.0, 5.0, (TOKENS, KEY_HEAD_WIDTH), jnp.float32)
    return jnp.concatenate([key_rows, value_rows], axis=1).astype(jnp.bfloat16)


def shard_levels(own_key, dims, shards, smallest, top_value):
    def one(dim, parts):
        heights = jax.random.uniform(jax.random.fold_in(jax.random.fold_in(own_key, 6), dim), (parts,), jnp.float32, smallest / len(shards), top_value / len(shards))
        return jnp.repeat(jnp.exp(heights), dims[dim] // parts).reshape((-1,) + (1,) * (len(dims) - dim - 1))

    level = one(*shards[0])
    for cut in shards[1:]:
        level = level * one(*cut)
    return level


def profile(number_of, total, bound, lean):
    weights = [(1 << 20) // math.isqrt(rank ** lean) + 1 for rank in range(2, number_of + 1)]
    rest, counts = total - bound - (number_of - 1), [1] * (number_of - 1)
    while rest > 0:
        candidates = [i for i in range(number_of - 1) if counts[i] < bound]
        mass, remaining = sum([weights[i] for i in candidates]), rest
        for i in candidates:
            more = min(bound - counts[i], max(1, remaining * weights[i] // mass), rest)
            counts[i] = counts[i] + more
            rest = rest - more
    return np.array([bound] + counts)


def uneven_parts(stream_key, count, total, bound, lean):
    if count == 2:
        one = jax.random.randint(stream_key, (), max(1, total - bound), min(bound, total - 1) + 1)
        return jnp.stack([one, total - one])
    sizes = jnp.asarray(profile(count, total, bound, lean), jnp.int32)
    twos = (count - 1) // 2
    giver, taker = sizes[1:1 + 2 * twos:2], sizes[2:2 + 2 * twos:2]
    slack = jnp.minimum(giver - 1, bound - taker)
    passed = jax.random.randint(jax.random.fold_in(stream_key, 1), (twos,), 0, 1 << 20) % (slack + 1)
    sizes = sizes.at[1:1 + 2 * twos:2].set(giver - passed).at[2:2 + 2 * twos:2].set(taker + passed)
    return sizes[jax.random.permutation(jax.random.fold_in(stream_key, 2), count)]


def scatter_about(own_key, dims, deviation, reach, cuts=(), kind=jnp.bfloat16):
    gain = shard_levels(own_key, dims, cuts, -0.22, 0.18) if cuts else 1.0
    array = jax.random.normal(own_key, dims, jnp.float32) * deviation * gain
    return jnp.minimum(jnp.maximum(array, -reach), reach).astype(kind)


def setup_inputs(seed: int = 0) -> dict:
    seeds = jax.random.split(jax.random.key(seed), 13)
    activations = scatter_about(seeds[0], (TOKENS, MODEL_WIDTH), 1.0, 6.0, ((0, 256),))
    queries = draw_queries(jax.random.fold_in(seeds[12], 71), 0)
    rotated_key_value = draw_rotated_key_value(jax.random.fold_in(seeds[12], 71), 0)
    attention_out_grad = scatter_about(seeds[3], (TOKENS, QW), 1.0, 6.0, ((0, 256),))
    adapter_down = scatter_about(seeds[4], (MODEL_WIDTH, 2 * ADAPTER_RANK), MODEL_WIDTH ** -0.5, 0.078125)
    adapter_up = scatter_about(seeds[5], (2 * ADAPTER_RANK, KEY_HEAD_WIDTH), ADAPTER_RANK ** -0.5, 0.75)
    bin_local_index = draw_bin_local_index(jax.random.fold_in(seeds[12], 71), 0)
    bin_row_offset = draw_bin_row_offset(jax.random.fold_in(seeds[12], 71), 0)
    spill_node = draw_spill_node(jax.random.fold_in(seeds[12], 71), 0)
    spill_row_offset = draw_spill_row_offset(jax.random.fold_in(seeds[12], 71), 0)
    arrival_pick_index = draw_arrival_pick_index(jax.random.fold_in(seeds[12], 71), 0)
    packed_sequence_number = jax.vmap(lambda own: jnp.searchsorted(jnp.cumsum(uneven_parts(own, 8, TOK_DEV, TOK_DEV // 2, 2)), jnp.arange(TOK_DEV), side="right"))(jax.random.split(seeds[11], BINS)).reshape((BINS, TOK_DEV)).astype(jnp.int32)
    return {"activations": activations, "queries": queries, "rotated_key_value": rotated_key_value, "attention_out_grad": attention_out_grad, "adapter_down": adapter_down, "adapter_up": adapter_up, "bin_local_index": bin_local_index, "bin_row_offset": bin_row_offset, "spill_node": spill_node, "spill_row_offset": spill_row_offset, "arrival_pick_index": arrival_pick_index, "packed_sequence_number": packed_sequence_number}


rope_theta = 1000000.0

def rope_tables(segments):
    slot_ids = jnp.arange(segments.shape[0], dtype=jnp.int32)
    seg_start = lax.optimization_barrier(jnp.sum((segments[None, :] < segments[:, None]).astype(jnp.int32), axis=1))
    position = (slot_ids - seg_start).astype(jnp.float32)
    frequency = rope_theta ** (-jnp.arange(0, HEAD, 2).astype(jnp.float32) / HEAD)
    angles = position[:, None] * frequency[None, :]
    return (jnp.cos(angles), jnp.sin(angles))

def unrotate(key_rot, cosine_table, sine_table):
    half_head = HEAD // 2
    first_half = key_rot[..., :half_head]
    second_half = key_rot[..., half_head:]
    cos_rows = cosine_table[:, None, :]
    sin_rows = sine_table[:, None, :]
    return jnp.concatenate([first_half * cos_rows + second_half * sin_rows, second_half * cos_rows - first_half * sin_rows], axis=-1)

def bin_backward(query_rows, kv_rows, grad_rows, segments):
    row_count = query_rows.shape[0]
    score_scale = 1.0 / jnp.sqrt(jnp.float32(HEAD))
    slot_ids = jnp.arange(row_count, dtype=jnp.int32)
    allowed = (segments[:, None] == segments[None, :]) & (slot_ids[None, :] <= slot_ids[:, None])
    query_heads = query_rows.astype(jnp.float32).reshape(row_count, KV_HEADS, GROUP, HEAD)
    grad_heads = grad_rows.astype(jnp.float32).reshape(row_count, KV_HEADS, GROUP, HEAD)
    key_part = kv_rows[:, :KEY_HEAD_WIDTH].astype(jnp.float32).reshape(row_count, KV_HEADS, HEAD)
    value_part = kv_rows[:, KEY_HEAD_WIDTH:].astype(jnp.float32).reshape(row_count, KV_HEADS, HEAD)
    scores = jnp.einsum('igsd,jgd->gsij', query_heads, key_part) * score_scale
    scores = jnp.where(allowed[None, None], scores, -jnp.inf)
    row_max = lax.optimization_barrier(jnp.max(scores, axis=-1, keepdims=True))
    weights = jnp.exp(scores - row_max)
    probs = weights / lax.optimization_barrier(jnp.sum(weights, axis=-1, keepdims=True))
    prob_grad = jnp.einsum('igsd,jgd->gsij', grad_heads, value_part)
    row_delta = lax.optimization_barrier(jnp.sum(probs * prob_grad, axis=-1, keepdims=True))
    score_grad = (probs * (prob_grad - row_delta)).astype(jnp.bfloat16)
    probs_low = probs.astype(jnp.bfloat16)
    probs_back = lax.optimization_barrier(probs_low).astype(jnp.float32)
    score_back = lax.optimization_barrier(score_grad).astype(jnp.float32)
    value_cotangent_rows = jnp.einsum('gsij,igsd->jgd', probs_back, grad_heads)
    key_rot = jnp.einsum('gsij,igsd->jgd', score_back, query_heads) * score_scale
    cosine_table, sine_table = rope_tables(segments)
    key_cotangent_rows = unrotate(key_rot, cosine_table, sine_table)
    return jnp.concatenate([key_cotangent_rows.reshape(row_count, KEY_HEAD_WIDTH), value_cotangent_rows.reshape(row_count, KEY_HEAD_WIDTH)], axis=1).astype(jnp.bfloat16)

def adapter_terms(active_rows, key_value_cotangent, adapter_down, adapter_up):
    key_cotangent_rows = key_value_cotangent[:, :KEY_HEAD_WIDTH]
    value_cotangent_rows = key_value_cotangent[:, KEY_HEAD_WIDTH:]
    raise_key = jnp.dot(key_cotangent_rows, adapter_up[:ADAPTER_RANK].T, preferred_element_type=jnp.float32)
    raise_value = jnp.dot(value_cotangent_rows, adapter_up[ADAPTER_RANK:].T, preferred_element_type=jnp.float32)
    lift = jnp.concatenate([raise_key, raise_value], axis=1).astype(jnp.bfloat16)
    down_factor_grad = jnp.dot(active_rows.T, lift, preferred_element_type=jnp.float32)
    down_product = jnp.dot(active_rows, adapter_down, preferred_element_type=jnp.float32).astype(jnp.bfloat16)
    up_key = jnp.dot(key_cotangent_rows.T, down_product[:, :ADAPTER_RANK], preferred_element_type=jnp.float32)
    up_value = jnp.dot(value_cotangent_rows.T, down_product[:, ADAPTER_RANK:], preferred_element_type=jnp.float32)
    return (down_factor_grad, jnp.concatenate([up_key, up_value], axis=1))

def reference(activations, queries, rotated_key_value, attention_out_grad, adapter_down, adapter_up, bin_local_index, bin_row_offset, spill_node, spill_row_offset, arrival_pick_index, packed_sequence_number):
    entries = TOK_DEV + N_LOCAL * CAP_L + N_NODE * CAP_N
    device = jnp.broadcast_to(jnp.arange(BINS, dtype=jnp.int32)[:, None], (BINS, TOK_DEV))
    row_ids = jnp.broadcast_to(jnp.arange(TOK_DEV, dtype=jnp.int32)[None, :], (BINS, TOK_DEV))
    dev_node = device // N_LOCAL
    dev_local = device % N_LOCAL
    moved_in = bin_local_index != dev_local
    moved_out = spill_node != dev_node
    dest_device = jnp.where(moved_in, dev_node * N_LOCAL + bin_local_index, jnp.where(moved_out, spill_node * N_LOCAL + dev_local, device))
    dest_entry = jnp.where(moved_in, TOK_DEV + dev_local * CAP_L + bin_row_offset, jnp.where(moved_out, TOK_DEV + N_LOCAL * CAP_L + dev_node * CAP_N + spill_row_offset, row_ids))
    source_ids = (device * TOK_DEV + row_ids).astype(jnp.int32)
    flat_dest = (dest_device * entries + dest_entry).astype(jnp.int32).reshape(-1)
    source_table = jnp.zeros((BINS * entries,), jnp.int32).at[flat_dest].set(source_ids.reshape(-1))
    bin_ids = jnp.arange(BINS, dtype=jnp.int32)[:, None]
    picks = source_table[(bin_ids * entries + arrival_pick_index).astype(jnp.int32).reshape(-1)].reshape(BINS, TOK_DEV)

    def one_bin(running, bin_inputs):
        select_rows, segments = bin_inputs
        key_value_cotangent = bin_backward(queries[select_rows], rotated_key_value[select_rows], attention_out_grad[select_rows], segments)
        down_contribution, up_contribution = adapter_terms(activations[select_rows], key_value_cotangent, adapter_down, adapter_up)
        return ((running[0] + down_contribution, running[1] + up_contribution), key_value_cotangent)
    start_sums = (jnp.zeros((MODEL_WIDTH, 2 * ADAPTER_RANK), jnp.float32), jnp.zeros((KEY_HEAD_WIDTH, 2 * ADAPTER_RANK), jnp.float32))
    totals, kv_grads = lax.scan(one_bin, start_sums, (picks, packed_sequence_number))
    factor = 1.0 / jnp.sqrt(jnp.float32(BINS * TOK_DEV))
    return (kv_grads.reshape(BINS * TOK_DEV, 2 * KEY_HEAD_WIDTH), totals[0] * factor, totals[1] * factor)
```

```python
import functools
import math

import numpy as np

import jax
import jax.numpy as jnp
from jax import lax
from jax.experimental import pallas as pl
from jax.experimental.pallas import tpu as pltpu
from jax.sharding import PartitionSpec as P

KV_HEADS = 8
HEAD = 128
ADAPTER_RANK = 64
CAP_L = 4
CAP_N = 4
GROUP = 5
KEY_HEAD_WIDTH = 1024
MODEL_WIDTH = 5120
ROWS = 256
PEERS = 16
MOVED = PEERS * CAP_L
ARRIVALS = ROWS + 2 * MOVED
ROPE_THETA = 1000000.0

QUARTERS = 4
GROUP_WIDTH = GROUP * HEAD
HEAD_COLS = 2 * GROUP_WIDTH + 2 * HEAD
HEAD_QUARTER = HEAD_COLS // QUARTERS
ATT_COLS = KV_HEADS * HEAD_QUARTER
X_QUARTER = MODEL_WIDTH // QUARTERS
LOG2E = math.log2(math.e)
BF = jnp.bfloat16
F32 = jnp.float32
MIB = 1 << 20
VMEM_LIMIT = 62 * MIB

DOWN_SHARD = 20
UP_SHARD = 4
SHARD = DOWN_SHARD + UP_SHARD
BLOCK_DEV = 32
BLOCK_COUNT = 8
DOWN_BLOCK = BLOCK_DEV * DOWN_SHARD
UP_BLOCK = BLOCK_DEV * UP_SHARD
BLOCK_ROWS = BLOCK_DEV * SHARD


def dot(a, b):
    return jnp.dot(a, b, preferred_element_type=F32)


def dot_nt(a, b):
    return lax.dot_general(a, b, (((1,), (1,)), ((), ())), preferred_element_type=F32)


def dot_tn(a, b):
    return lax.dot_general(a, b, (((0,), (0,)), ((), ())), preferred_element_type=F32)


def iota(shape, dim):
    return lax.broadcasted_iota(jnp.int32, shape, dim)


def interleave(rows, scratch):
    blocks = scratch.shape[0]
    for c in range(QUARTERS):
        for i in range(blocks):
            at = (c * blocks + i) * HEAD
            scratch[i, pl.ds(c, MOVED, stride=QUARTERS), :] = rows[:, at : at + HEAD]
    wide = jnp.concatenate([scratch[i] for i in range(blocks)], axis=1)
    return wide.astype(BF).reshape(PEERS, 16, blocks * HEAD)


def gather_quarters(rows, scratch):
    blocks = scratch.shape[0]
    wide = rows.reshape(ROWS, blocks * HEAD).astype(F32)
    for i in range(blocks):
        scratch[i] = wide[:, i * HEAD : (i + 1) * HEAD]
    return jnp.concatenate(
        [
            scratch[i, pl.ds(c, MOVED, stride=QUARTERS), :]
            for c in range(QUARTERS)
            for i in range(blocks)
        ],
        axis=1,
    ).astype(BF)


X_STEPS = 5
X_STEP = X_QUARTER // X_STEPS


def columns(j, width):
    return slice(j * width, (j + 1) * width)


def pack_kernel(near, target, q, g, kv, x, *rest):
    if near:
        att_out, *rest = rest
        x_out, x_from = att_out, ATT_COLS
    else:
        down, att_out, x_out, down_out, *rest = rest
        x_from = 0
    q_in, g_in, kv_in, x_in, att, att_x, spread, spread_x, head_sem, x_sem, out_sem, *rest = rest

    loads = [pltpu.make_async_copy(kv, kv_in, head_sem.at[2 * KV_HEADS])]
    for j in range(KV_HEADS):
        part = columns(j, GROUP_WIDTH)
        loads.append(pltpu.make_async_copy(q.at[:, part], q_in.at[:, part], head_sem.at[2 * j]))
        loads.append(
            pltpu.make_async_copy(g.at[:, part], g_in.at[:, part], head_sem.at[2 * j + 1])
        )
    x_loads = []
    for c in range(QUARTERS):
        part = columns(c, X_QUARTER)
        x_loads.append(pltpu.make_async_copy(x.at[:, part], x_in.at[:, part], x_sem.at[c]))
    if not near:
        down_in, att_down, down_sem = rest
        x_loads.append(pltpu.make_async_copy(down, down_in, down_sem.at[0]))
    for load in loads + x_loads:
        load.start()

    select = jnp.where(iota((MOVED, ROWS), 0) == target[...], 1.0, 0.0).astype(BF)
    stores = []

    def send(source, to, sem):
        stores.append(pltpu.make_async_copy(source, to, sem))
        stores[-1].start()

    loads[0].wait()
    for j in range(KV_HEADS):
        loads[1 + 2 * j].wait()
        loads[2 + 2 * j].wait()
        part = columns(j, GROUP_WIDTH)
        rows = jnp.concatenate(
            [
                q_in[:, part],
                g_in[:, part],
                kv_in[:, columns(j, HEAD)],
                kv_in[:, columns(KV_HEADS + j, HEAD)],
            ],
            axis=1,
        )
        part = columns(j, HEAD_QUARTER)
        att[:, :, part] = interleave(dot(select, rows), spread.at[j % 2])
        send(att.at[:, :, part], att_out.at[:, :, part], out_sem.at[j])
    for load in x_loads:
        load.wait()
    for j in range(X_STEPS):
        rows = jnp.concatenate(
            [x_in[:, columns(c * X_STEPS + j, X_STEP)] for c in range(QUARTERS)], axis=1
        )
        part = columns(j, X_STEP)
        att_x[:, :, part] = interleave(dot(select, rows), spread_x.at[j % 2])
        to = slice(x_from + part.start, x_from + part.stop)
        send(att_x.at[:, :, part], x_out.at[:, :, to], out_sem.at[KV_HEADS + j])
    if not near:
        own_out = dot(x_in[...], down_in[...]).astype(BF)
        down_out[...] = own_out
        picked = dot(select, own_out)
        rows = jnp.concatenate([picked] + [jnp.zeros_like(picked)] * (QUARTERS - 1), axis=1)
        att_down[...] = interleave(rows, spread_x.at[0, :1])
        send(att_down, x_out.at[:, :, X_QUARTER:], down_sem.at[1])
    for store in stores:
        store.wait()


def pack(target, queries, grads, kv, activations, down=None):
    near = down is None
    hbm, vmem = pl.BlockSpec(memory_space=pltpu.HBM), pl.BlockSpec(memory_space=pltpu.VMEM)
    scratch = [
        pltpu.VMEM((ROWS, KV_HEADS * GROUP_WIDTH), BF),
        pltpu.VMEM((ROWS, KV_HEADS * GROUP_WIDTH), BF),
        pltpu.VMEM((ROWS, 2 * KEY_HEAD_WIDTH), BF),
        pltpu.VMEM((ROWS, MODEL_WIDTH), BF),
        pltpu.VMEM((PEERS, 16, ATT_COLS), BF),
        pltpu.VMEM((PEERS, 16, X_QUARTER), BF),
        pltpu.VMEM((2, HEAD_QUARTER // HEAD, ROWS, HEAD), F32),
        pltpu.VMEM((2, X_STEP // HEAD, ROWS, HEAD), F32),
        pltpu.SemaphoreType.DMA((2 * KV_HEADS + 1,)),
        pltpu.SemaphoreType.DMA((QUARTERS,)),
        pltpu.SemaphoreType.DMA((KV_HEADS + X_STEPS,)),
    ]
    if near:
        args, out_specs = (), [hbm]
        out_shape = [jax.ShapeDtypeStruct((PEERS, 16, ATT_COLS + X_QUARTER), BF)]
    else:
        args, out_specs = (down,), [hbm, hbm, vmem]
        out_shape = [
            jax.ShapeDtypeStruct((PEERS, 16, ATT_COLS), BF),
            jax.ShapeDtypeStruct((PEERS, 16, X_QUARTER + HEAD), BF),
            jax.ShapeDtypeStruct((ROWS, HEAD), BF),
        ]
        scratch += [
            pltpu.VMEM((MODEL_WIDTH, HEAD), BF),
            pltpu.VMEM((PEERS, 16, HEAD), BF),
            pltpu.SemaphoreType.DMA((2,)),
        ]
    return pl.pallas_call(
        functools.partial(pack_kernel, near),
        in_specs=[vmem] + [hbm] * (4 + len(args)),
        out_specs=out_specs,
        out_shape=out_shape,
        scratch_shapes=scratch,
        compiler_params=pltpu.CompilerParams(vmem_limit_bytes=VMEM_LIMIT),
        cost_estimate=pl.CostEstimate(
            flops=2 * MOVED * ROWS * QUARTERS * (ATT_COLS + X_QUARTER),
            bytes_accessed=14 * MIB,
            transcendentals=0,
        ),
        name="pack_rows",
    )(target, queries, grads, kv, activations, *args)


def near_kernel(near, down, x_out, down_out, spread):
    rows = gather_quarters(near[...], spread)
    x_out[...] = rows
    down_out[...] = dot(rows, down[...]).astype(BF)


def near_adapter_rows(near, down):
    return pl.pallas_call(
        near_kernel,
        grid=(1,),
        in_specs=[
            pl.BlockSpec((PEERS, 16, X_QUARTER), lambda i: (0, 0, 0)),
            pl.BlockSpec((MODEL_WIDTH, HEAD), lambda i: (0, 0)),
        ],
        out_specs=[
            pl.BlockSpec((MOVED, MODEL_WIDTH), lambda i: (0, 0)),
            pl.BlockSpec((MOVED, HEAD), lambda i: (0, 0)),
        ],
        out_shape=[
            jax.ShapeDtypeStruct((MOVED, MODEL_WIDTH), BF),
            jax.ShapeDtypeStruct((MOVED, HEAD), BF),
        ],
        scratch_shapes=[pltpu.VMEM((X_QUARTER // HEAD, ROWS, HEAD), F32)],
        compiler_params=pltpu.CompilerParams(vmem_limit_bytes=VMEM_LIMIT),
        cost_estimate=pl.CostEstimate(
            flops=2 * MOVED * MODEL_WIDTH * HEAD, bytes_accessed=3 * MIB, transcendentals=0
        ),
        name="near_adapter_rows",
    )(near, down)


def arrival_pick(pick, entry):
    return jnp.where(pick == entry, 1.0, 0.0).astype(BF)


def attention_kernel(
    pick_col, seg_row, seg_col, cos, sin, up, q, g, k, v, near, far, grad_out, lift_out,
    gather, bias, lift, spread, spread_far
):
    step = pl.program_id(0)

    @pl.when(step == 0)
    def _():
        gather[...] = arrival_pick(pick_col[...], iota((ROWS, ARRIVALS), 1))
        allowed = (seg_col[...] == seg_row[...]) & (
            iota((ROWS, ROWS), 0) <= iota((ROWS, ROWS), 1)
        )
        bias[...] = jnp.where(allowed, 0.0, -1e30)
        lift[...] = jnp.zeros_like(lift)

    columns = jnp.concatenate([q[...], g[...], k[...], v[...]], axis=1)
    near_rows = gather_quarters(near[...], spread)
    far_rows = gather_quarters(far[...], spread_far)
    packed = dot(gather[...], jnp.concatenate([columns, near_rows, far_rows], axis=0)).astype(BF)
    key = packed[:, 2 * GROUP_WIDTH : 2 * GROUP_WIDTH + HEAD]
    value = packed[:, 2 * GROUP_WIDTH + HEAD :]
    score_scale = 1.0 / math.sqrt(HEAD)

    half = ROWS // 2
    sums = []
    for block in range(2):
        rows = slice(block * half, (block + 1) * half)
        keys = (block + 1) * half
        query = jnp.concatenate(
            [packed[rows, h * HEAD : (h + 1) * HEAD] for h in range(GROUP)], axis=0
        )
        grad = jnp.concatenate(
            [packed[rows, GROUP_WIDTH + h * HEAD : GROUP_WIDTH + (h + 1) * HEAD] for h in range(GROUP)],
            axis=0,
        )
        block_bias = jnp.concatenate([bias[:keys, rows]] * GROUP, axis=1)
        scores = dot_nt(key[:keys], query) * (score_scale * LOG2E) + block_bias
        weights = jnp.exp2(scores - jnp.max(scores, axis=0, keepdims=True))
        probs = weights * (1.0 / jnp.sum(weights, axis=0, keepdims=True))
        prob_grad = dot_nt(value[:keys], grad)
        delta = jnp.sum(probs * prob_grad, axis=0, keepdims=True)
        score_grad = (probs * (prob_grad - delta)).astype(BF)
        sums.append((dot(score_grad, query), dot(probs.astype(BF), grad)))
    key_rot = jnp.concatenate([sums[0][0] + sums[1][0][:half], sums[1][0][half:]], axis=0)
    value_grad = jnp.concatenate([sums[0][1] + sums[1][1][:half], sums[1][1][half:]], axis=0)
    key_rot = key_rot * score_scale
    swapped = jnp.concatenate([key_rot[:, HEAD // 2 :], key_rot[:, : HEAD // 2]], axis=1)
    key_grad = key_rot * cos[...] + swapped * sin[...]

    key_grad = key_grad.astype(BF)
    value_grad = value_grad.astype(BF)
    grad_out[:, pl.ds(pl.multiple_of(step * HEAD, HEAD), HEAD)] = key_grad
    grad_out[:, pl.ds(pl.multiple_of(KEY_HEAD_WIDTH + step * HEAD, HEAD), HEAD)] = value_grad
    up_rows = up[...]
    zero = jnp.zeros((ADAPTER_RANK, HEAD), BF)
    key_up = jnp.concatenate([up_rows[:ADAPTER_RANK], zero], axis=0)
    value_up = jnp.concatenate([zero, up_rows[ADAPTER_RANK:]], axis=0)
    lift[...] += dot_nt(
        jnp.concatenate([key_grad, value_grad], axis=1),
        jnp.concatenate([key_up, value_up], axis=1),
    )

    @pl.when(step == KV_HEADS - 1)
    def _():
        lift_out[...] = lift[...].astype(BF)


def attention(pick_col, seg_row, seg_col, cos, sin, up, queries, grads, kv, near, far):
    def whole(shape):
        return pl.BlockSpec(shape, lambda j: (0,) * len(shape))

    def head_block(width):
        return pl.BlockSpec((ROWS, width), lambda j: (0, j))

    arrived = pl.BlockSpec((PEERS, 16, HEAD_QUARTER), lambda j: (0, 0, j))
    return pl.pallas_call(
        attention_kernel,
        grid=(KV_HEADS,),
        in_specs=[
            whole((ROWS, 1)),
            whole((1, ROWS)),
            whole((ROWS, 1)),
            whole((ROWS, HEAD)),
            whole((ROWS, HEAD)),
            pl.BlockSpec((2 * ADAPTER_RANK, HEAD), lambda j: (0, j)),
            head_block(GROUP_WIDTH),
            head_block(GROUP_WIDTH),
            head_block(HEAD),
            pl.BlockSpec((ROWS, HEAD), lambda j: (0, KV_HEADS + j)),
            arrived,
            arrived,
        ],
        out_specs=[whole((ROWS, 2 * KEY_HEAD_WIDTH)), whole((ROWS, HEAD))],
        out_shape=[
            jax.ShapeDtypeStruct((ROWS, 2 * KEY_HEAD_WIDTH), BF),
            jax.ShapeDtypeStruct((ROWS, HEAD), BF),
        ],
        scratch_shapes=[
            pltpu.VMEM((ROWS, ARRIVALS), BF),
            pltpu.VMEM((ROWS, ROWS), F32),
            pltpu.VMEM((ROWS, HEAD), F32),
            pltpu.VMEM((HEAD_QUARTER // HEAD, ROWS, HEAD), F32),
            pltpu.VMEM((HEAD_QUARTER // HEAD, ROWS, HEAD), F32),
        ],
        compiler_params=pltpu.CompilerParams(vmem_limit_bytes=VMEM_LIMIT),
        cost_estimate=pl.CostEstimate(
            flops=12 * 10**9, bytes_accessed=14 * MIB, transcendentals=2 * 10**6
        ),
        name="attention_grads",
    )(pick_col, seg_row, seg_col, cos, sin, up, queries, grads, kv, kv, near, far)


def adapter_kernel(
    pick_row, pick_col, order_col, lift, own_down, near_down, near_x, far, x, kv_grad, out,
    x_in, kv_in, far_in, near_in, placed_out, spread, load_sem, out_sem
):
    loads = [
        pltpu.make_async_copy(far, far_in, load_sem.at[0]),
        pltpu.make_async_copy(kv_grad, kv_in, load_sem.at[1]),
        pltpu.make_async_copy(near_x, near_in, load_sem.at[2]),
    ]
    for c in range(QUARTERS):
        part = columns(c, X_QUARTER)
        loads.append(pltpu.make_async_copy(x.at[:, part], x_in.at[:, part], load_sem.at[3 + c]))
    for load in loads:
        load.start()

    order = jnp.where(iota((BLOCK_ROWS, BLOCK_ROWS), 1) == order_col[...], 1.0, 0.0).astype(BF)
    gather = arrival_pick(pick_col[...], iota((ROWS, ARRIVALS), 1))
    spread_lift = arrival_pick(pick_row[...], iota((ARRIVALS, ROWS), 0))
    lifted = dot(spread_lift, lift[...]).astype(BF)

    loads[0].wait()
    far_rows = gather_quarters(far_in[:, :, :X_QUARTER], spread)
    spread[0] = far_in[:, :, X_QUARTER:].reshape(ROWS, HEAD).astype(F32)
    far_down = spread[0, pl.ds(0, MOVED, stride=QUARTERS), :].astype(BF)

    arrived_down = jnp.concatenate([own_down[...], near_down[...], far_down], axis=0)
    down_out = dot(gather, arrived_down).astype(BF)
    loads[1].wait()
    up_both = dot_tn(down_out, kv_in[...])
    up_sum = jnp.concatenate(
        [up_both[:ADAPTER_RANK, :KEY_HEAD_WIDTH], up_both[ADAPTER_RANK:, KEY_HEAD_WIDTH:]], axis=0
    ).astype(BF)

    loads[2].wait()
    stores = []
    for z_lo in range(BLOCK_COUNT // 2):
        part = columns(z_lo, X_QUARTER)
        loads[3 + z_lo].wait()
        arrived = jnp.concatenate([x_in[:, part], near_in[:, part], far_rows[:, part]], axis=0)
        down_sum = dot_tn(lifted, arrived).astype(BF)
        both = jnp.concatenate(
            [
                jnp.concatenate(
                    [
                        down_sum[:, columns(y_high, DOWN_BLOCK)],
                        up_sum[:, columns(2 * z_lo + y_high, UP_BLOCK)],
                    ],
                    axis=1,
                )
                for y_high in range(2)
            ],
            axis=0,
        )
        placed = dot_nt(order, both).astype(BF)
        rows = columns(z_lo, 2 * SHARD)
        for y_high in range(2):
            for c in range(2):
                for xx in range(4):
                    for y_low in range(2):
                        at = ((c * 4 + xx) * 2 + y_low) * 2 * SHARD
                        placed_out[c, xx * 4 + y_high * 2 + y_low, rows, :] = placed[
                            at : at + 2 * SHARD, columns(y_high, HEAD)
                        ]
        stores.append(
            pltpu.make_async_copy(
                placed_out.at[:, :, rows], out.at[:, :, rows], out_sem.at[z_lo]
            )
        )
        stores[-1].start()
    for store in stores:
        store.wait()


def shard_order():
    order = []
    for c in range(2):
        for xx in range(4):
            for y_low in range(2):
                for z_hi in range(2):
                    device = ((y_low * 4 + xx) * 2 + z_hi) * 2 + c
                    for r in range(DOWN_SHARD):
                        order.append(device * DOWN_SHARD + r)
                    for r in range(UP_SHARD):
                        order.append(DOWN_BLOCK + device * UP_SHARD + r)
    return np.asarray(order, np.int32).reshape(BLOCK_ROWS, 1)


def adapters(pick_row, pick_col, lift, own_down, near_down, near_x, far, x, kv_grad):
    hbm, vmem = pl.BlockSpec(memory_space=pltpu.HBM), pl.BlockSpec(memory_space=pltpu.VMEM)
    order_col = jnp.asarray(shard_order())
    return pl.pallas_call(
        adapter_kernel,
        out_shape=jax.ShapeDtypeStruct((2, 16, 8 * SHARD, HEAD), BF),
        in_specs=[vmem] * 6 + [hbm] * 4,
        out_specs=hbm,
        scratch_shapes=[
            pltpu.VMEM((ROWS, MODEL_WIDTH), BF),
            pltpu.VMEM((ROWS, 2 * KEY_HEAD_WIDTH), BF),
            pltpu.VMEM((PEERS, 16, X_QUARTER + HEAD), BF),
            pltpu.VMEM((MOVED, MODEL_WIDTH), BF),
            pltpu.VMEM((2, 16, 8 * SHARD, HEAD), BF),
            pltpu.VMEM((X_QUARTER // HEAD, ROWS, HEAD), F32),
            pltpu.SemaphoreType.DMA((3 + QUARTERS,)),
            pltpu.SemaphoreType.DMA((BLOCK_COUNT // 2,)),
        ],
        compiler_params=pltpu.CompilerParams(vmem_limit_bytes=VMEM_LIMIT),
        cost_estimate=pl.CostEstimate(
            flops=4 * 10**9, bytes_accessed=10 * MIB, transcendentals=0
        ),
        name="adapter_grads",
    )(pick_row, pick_col, order_col, lift, own_down, near_down, near_x, far, x, kv_grad)


def device_groups(axes):
    names = ["z_lo", "y", "x", "z_hi", "core"]
    index = np.arange(256).reshape(4, 4, 4, 2, 2)
    moved = [names.index(a) for a in axes]
    rest = [i for i in range(5) if i not in moved]
    size = math.prod(index.shape[i] for i in moved)
    return index.transpose(rest + moved).reshape(-1, size).tolist()


def exchange(array, axes):
    return lax.all_to_all(
        array,
        ("node", "local"),
        split_axis=0,
        concat_axis=0,
        axis_index_groups=device_groups(axes),
        tiled=True,
    )


def sum_over_devices(parts):
    both = exchange(parts, ["core"])
    total = (both[0].astype(F32) + both[1].astype(F32)).astype(BF)
    total = jnp.sum(exchange(total, ["x", "y"]).astype(F32), axis=0)
    total = total.reshape(8, SHARD, HEAD)
    return jnp.sum(exchange(total, ["z_lo", "z_hi"]), axis=0)


def rope_tables(segments):
    slot_ids = jnp.arange(segments.shape[0], dtype=jnp.int32)
    seg_start = jnp.sum((segments[None, :] < segments[:, None]).astype(jnp.int32), axis=1)
    position = (slot_ids - seg_start).astype(F32)
    frequency = ROPE_THETA ** (-jnp.arange(0, HEAD, 2).astype(F32) / HEAD)
    angles = position[:, None] * frequency[None, :]
    cosine, sine = jnp.cos(angles), jnp.sin(angles)
    return (
        jnp.concatenate([cosine, cosine], axis=1),
        jnp.concatenate([sine, -sine], axis=1),
    )


def local(
    activations,
    queries,
    rotated_key_value,
    attention_out_grad,
    adapter_down,
    adapter_up,
    bin_local_index,
    bin_row_offset,
    spill_node,
    spill_row_offset,
    arrival_pick_index,
    packed_sequence_number,
):
    own_local = lax.axis_index("local")
    own_node = lax.axis_index("node")
    moved_in = bin_local_index != own_local
    moved_out = jnp.logical_not(moved_in) & (spill_node != own_node)
    near_target = jnp.where(moved_in, bin_local_index * CAP_L + bin_row_offset, -1)
    far_target = jnp.where(moved_out, spill_node * CAP_N + spill_row_offset, -1)

    rows = (queries, attention_out_grad, rotated_key_value, activations)
    (near_send,) = pack(near_target, *rows)
    far_send, far_x_send, own_down = pack(far_target, *rows, adapter_down)

    near = lax.all_to_all(near_send, "local", split_axis=0, concat_axis=0, tiled=True)
    far_send, near = lax.optimization_barrier((far_send, near))
    far = lax.all_to_all(far_send, "node", split_axis=0, concat_axis=0, tiled=True)
    near_x, near_down = near_adapter_rows(near[:, :, ATT_COLS:], adapter_down)
    pick_row = arrival_pick_index
    pick_col = arrival_pick_index.reshape(ROWS, 1)
    seg_row = packed_sequence_number
    seg_col = packed_sequence_number.reshape(ROWS, 1)
    cos, sin = rope_tables(packed_sequence_number.reshape(-1))
    far_x_send, far, near_x, near_down, pick_col, seg_col, cos, sin = lax.optimization_barrier(
        (far_x_send, far, near_x, near_down, pick_col, seg_col, cos, sin)
    )
    far_x = lax.all_to_all(far_x_send, "node", split_axis=0, concat_axis=0, tiled=True)

    kv_grad, lift = attention(
        pick_col,
        seg_row,
        seg_col,
        cos,
        sin,
        adapter_up,
        queries,
        attention_out_grad,
        rotated_key_value,
        near,
        far,
    )
    parts = adapters(
        pick_row,
        pick_col,
        lift,
        own_down,
        near_down,
        near_x,
        far_x,
        activations,
        kv_grad,
    )
    total = sum_over_devices(parts) * (1.0 / math.sqrt(256 * ROWS))
    return (kv_grad, total[:DOWN_SHARD], total[DOWN_SHARD:])


def solution(mesh):
    split = P(("node", "local"), None)
    return jax.shard_map(
        local,
        mesh=mesh,
        in_specs=(split,) * 4 + (P(), P()) + (split,) * 6,
        out_specs=(split,) * 3,
        check_vma=False,
    )
```

```python
import functools
import math

import numpy as np

import jax
import jax.numpy as jnp
from jax import lax
from jax.experimental import pallas as pl
from jax.experimental.pallas import tpu as pltpu
from jax.sharding import PartitionSpec as P

KV_HEADS = 8
HEAD = 128
ADAPTER_RANK = 64
CAP_L = 4
CAP_N = 4
GROUP = 5
KEY_HEAD_WIDTH = 1024
MODEL_WIDTH = 5120
ROWS = 256
PEERS = 16
MOVED = PEERS * CAP_L
ARRIVALS = ROWS + 2 * MOVED
ROPE_THETA = 1000000.0

QUARTERS = 4
GROUP_WIDTH = GROUP * HEAD
HEAD_COLS = 2 * GROUP_WIDTH + 2 * HEAD
HEAD_QUARTER = HEAD_COLS // QUARTERS
ATT_COLS = KV_HEADS * HEAD_QUARTER
X_QUARTER = MODEL_WIDTH // QUARTERS
LOG2E = math.log2(math.e)
BF = jnp.bfloat16
F32 = jnp.float32
MIB = 1 << 20
VMEM_LIMIT = 62 * MIB

DOWN_SHARD = 20
UP_SHARD = 4
SHARD = DOWN_SHARD + UP_SHARD
BLOCK_DEV = 32
BLOCK_COUNT = 8
DOWN_BLOCK = BLOCK_DEV * DOWN_SHARD
UP_BLOCK = BLOCK_DEV * UP_SHARD
PARTS = 4
PART_ROWS = 4 * SHARD
PART_COLS = 3 * HEAD
PART_SHIFT = 32


def dot(a, b):
    return jnp.dot(a, b, preferred_element_type=F32)


def dot_nt(a, b):
    return lax.dot_general(a, b, (((1,), (1,)), ((), ())), preferred_element_type=F32)


def dot_tn(a, b):
    return lax.dot_general(a, b, (((0,), (0,)), ((), ())), preferred_element_type=F32)


def iota(shape, dim):
    return lax.broadcasted_iota(jnp.int32, shape, dim)


def interleave(rows, scratch):
    blocks = scratch.shape[0]
    for c in range(QUARTERS):
        for i in range(blocks):
            at = (c * blocks + i) * HEAD
            scratch[i, pl.ds(c, MOVED, stride=QUARTERS), :] = rows[:, at : at + HEAD]
    wide = jnp.concatenate([scratch[i] for i in range(blocks)], axis=1)
    return wide.astype(BF).reshape(PEERS, 16, blocks * HEAD)


def gather_quarters(rows, scratch):
    blocks = scratch.shape[0]
    wide = rows.reshape(ROWS, blocks * HEAD).astype(F32)
    for i in range(blocks):
        scratch[i] = wide[:, i * HEAD : (i + 1) * HEAD]
    return jnp.concatenate(
        [
            scratch[i, pl.ds(c, MOVED, stride=QUARTERS), :]
            for c in range(QUARTERS)
            for i in range(blocks)
        ],
        axis=1,
    ).astype(BF)


X_STEPS = 5
X_STEP = X_QUARTER // X_STEPS


def columns(j, width):
    return slice(j * width, (j + 1) * width)


def pack_kernel(near, bin_local, bin_offset, spill_node, spill_offset, q, g, kv, x, *rest):
    if near:
        att_out, *rest = rest
        x_out, x_from = att_out, ATT_COLS
    else:
        down, att_out, x_out, down_out, *rest = rest
        x_from = 0
    q_in, g_in, kv_in, x_in, att, att_x, spread, spread_x, head_sem, x_sem, out_sem, *rest = rest

    loads = [pltpu.make_async_copy(kv, kv_in, head_sem.at[2 * KV_HEADS])]
    for j in range(KV_HEADS):
        part = columns(j, GROUP_WIDTH)
        loads.append(pltpu.make_async_copy(q.at[:, part], q_in.at[:, part], head_sem.at[2 * j]))
        loads.append(
            pltpu.make_async_copy(g.at[:, part], g_in.at[:, part], head_sem.at[2 * j + 1])
        )
    x_loads = []
    for c in range(QUARTERS):
        part = columns(c, X_QUARTER)
        x_loads.append(pltpu.make_async_copy(x.at[:, part], x_in.at[:, part], x_sem.at[c]))
    if not near:
        down_in, att_down, down_sem = rest
        x_loads.append(pltpu.make_async_copy(down, down_in, down_sem.at[0]))
    for load in loads + x_loads:
        load.start()

    stays_in = bin_local[...] == lax.axis_index("local")
    if near:
        target = jnp.where(stays_in, -1, bin_local[...] * CAP_L + bin_offset[...])
    else:
        moves = stays_in & (spill_node[...] != lax.axis_index("node"))
        target = jnp.where(moves, spill_node[...] * CAP_N + spill_offset[...], -1)
    select = jnp.where(iota((MOVED, ROWS), 0) == target, 1.0, 0.0).astype(BF)
    stores = []

    def send(source, to, sem):
        stores.append(pltpu.make_async_copy(source, to, sem))
        stores[-1].start()

    loads[0].wait()
    for j in range(KV_HEADS):
        loads[1 + 2 * j].wait()
        loads[2 + 2 * j].wait()
        part = columns(j, GROUP_WIDTH)
        rows = jnp.concatenate(
            [
                q_in[:, part],
                g_in[:, part],
                kv_in[:, columns(j, HEAD)],
                kv_in[:, columns(KV_HEADS + j, HEAD)],
            ],
            axis=1,
        )
        part = columns(j, HEAD_QUARTER)
        att[:, :, part] = interleave(dot(select, rows), spread.at[j % 2])
        send(att.at[:, :, part], att_out.at[:, :, part], out_sem.at[j])
    for load in x_loads:
        load.wait()
    for j in range(X_STEPS):
        rows = jnp.concatenate(
            [x_in[:, columns(c * X_STEPS + j, X_STEP)] for c in range(QUARTERS)], axis=1
        )
        part = columns(j, X_STEP)
        att_x[:, :, part] = interleave(dot(select, rows), spread_x.at[j % 2])
        to = slice(x_from + part.start, x_from + part.stop)
        send(att_x.at[:, :, part], x_out.at[:, :, to], out_sem.at[KV_HEADS + j])
    if not near:
        own_out = dot(x_in[...], down_in[...]).astype(BF)
        down_out[...] = own_out
        picked = dot(select, own_out)
        rows = jnp.concatenate([picked] + [jnp.zeros_like(picked)] * (QUARTERS - 1), axis=1)
        att_down[...] = interleave(rows, spread_x.at[0, :1])
        send(att_down, x_out.at[:, :, X_QUARTER:], down_sem.at[1])
    for store in stores:
        store.wait()


def pack(plan, queries, grads, kv, activations, down=None):
    near = down is None
    hbm, vmem = pl.BlockSpec(memory_space=pltpu.HBM), pl.BlockSpec(memory_space=pltpu.VMEM)
    scratch = [
        pltpu.VMEM((ROWS, KV_HEADS * GROUP_WIDTH), BF),
        pltpu.VMEM((ROWS, KV_HEADS * GROUP_WIDTH), BF),
        pltpu.VMEM((ROWS, 2 * KEY_HEAD_WIDTH), BF),
        pltpu.VMEM((ROWS, MODEL_WIDTH), BF),
        pltpu.VMEM((PEERS, 16, ATT_COLS), BF),
        pltpu.VMEM((PEERS, 16, X_QUARTER), BF),
        pltpu.VMEM((2, HEAD_QUARTER // HEAD, ROWS, HEAD), F32),
        pltpu.VMEM((2, X_STEP // HEAD, ROWS, HEAD), F32),
        pltpu.SemaphoreType.DMA((2 * KV_HEADS + 1,)),
        pltpu.SemaphoreType.DMA((QUARTERS,)),
        pltpu.SemaphoreType.DMA((KV_HEADS + X_STEPS,)),
    ]
    if near:
        args, out_specs = (), [hbm]
        out_shape = [jax.ShapeDtypeStruct((PEERS, 16, ATT_COLS + X_QUARTER), BF)]
    else:
        args, out_specs = (down,), [hbm, hbm, vmem]
        out_shape = [
            jax.ShapeDtypeStruct((PEERS, 16, ATT_COLS), BF),
            jax.ShapeDtypeStruct((PEERS, 16, X_QUARTER + HEAD), BF),
            jax.ShapeDtypeStruct((ROWS, HEAD), BF),
        ]
        scratch += [
            pltpu.VMEM((MODEL_WIDTH, HEAD), BF),
            pltpu.VMEM((PEERS, 16, HEAD), BF),
            pltpu.SemaphoreType.DMA((2,)),
        ]
    return pl.pallas_call(
        functools.partial(pack_kernel, near),
        in_specs=[vmem] * 4 + [hbm] * (4 + len(args)),
        out_specs=out_specs,
        out_shape=out_shape,
        scratch_shapes=scratch,
        compiler_params=pltpu.CompilerParams(vmem_limit_bytes=VMEM_LIMIT),
        cost_estimate=pl.CostEstimate(
            flops=2 * MOVED * ROWS * QUARTERS * (ATT_COLS + X_QUARTER),
            bytes_accessed=14 * MIB,
            transcendentals=0,
        ),
        name="pack_rows",
    )(*plan, queries, grads, kv, activations, *args)


def near_kernel(near, down, x_out, down_out, spread):
    rows = gather_quarters(near[...], spread)
    x_out[...] = rows
    down_out[...] = dot(rows, down[...]).astype(BF)


def near_adapter_rows(near, down):
    return pl.pallas_call(
        near_kernel,
        grid=(1,),
        in_specs=[
            pl.BlockSpec((PEERS, 16, X_QUARTER), lambda i: (0, 0, 0)),
            pl.BlockSpec((MODEL_WIDTH, HEAD), lambda i: (0, 0)),
        ],
        out_specs=[
            pl.BlockSpec((MOVED, MODEL_WIDTH), lambda i: (0, 0)),
            pl.BlockSpec((MOVED, HEAD), lambda i: (0, 0)),
        ],
        out_shape=[
            jax.ShapeDtypeStruct((MOVED, MODEL_WIDTH), BF),
            jax.ShapeDtypeStruct((MOVED, HEAD), BF),
        ],
        scratch_shapes=[pltpu.VMEM((X_QUARTER // HEAD, ROWS, HEAD), F32)],
        compiler_params=pltpu.CompilerParams(vmem_limit_bytes=VMEM_LIMIT),
        cost_estimate=pl.CostEstimate(
            flops=2 * MOVED * MODEL_WIDTH * HEAD, bytes_accessed=3 * MIB, transcendentals=0
        ),
        name="near_adapter_rows",
    )(near, down)


def to_column(row):
    diagonal = iota((ROWS, ROWS), 0) == iota((ROWS, ROWS), 1)
    return jnp.sum(jnp.where(diagonal, row, 0), axis=1, keepdims=True)


def arrival_pick(pick, entry):
    return jnp.where(pick == entry, 1.0, 0.0).astype(BF)


STEP_HEADS = 2


def head_grads(
    step, i, up, q, g, k, v, near, far, grad_out, gather, bias, lift, spread, spread_far, cos, sin
):
    part, wide = columns(i, HEAD), columns(i, GROUP_WIDTH)
    own_rows = jnp.concatenate([q[:, wide], g[:, wide], k[:, part], v[:, part]], axis=1)
    near_rows = gather_quarters(near[:, :, columns(i, HEAD_QUARTER)], spread.at[i])
    far_rows = gather_quarters(far[:, :, columns(i, HEAD_QUARTER)], spread_far.at[i])
    packed = dot(gather[...], jnp.concatenate([own_rows, near_rows, far_rows], axis=0)).astype(BF)
    key = packed[:, 2 * GROUP_WIDTH : 2 * GROUP_WIDTH + HEAD]
    value = packed[:, 2 * GROUP_WIDTH + HEAD :]
    score_scale = 1.0 / math.sqrt(HEAD)

    half = ROWS // 2
    sums = []
    for block in range(2):
        rows = slice(block * half, (block + 1) * half)
        keys = (block + 1) * half
        query = jnp.concatenate(
            [packed[rows, h * HEAD : (h + 1) * HEAD] for h in range(GROUP)], axis=0
        )
        grad = jnp.concatenate(
            [packed[rows, GROUP_WIDTH + h * HEAD : GROUP_WIDTH + (h + 1) * HEAD] for h in range(GROUP)],
            axis=0,
        )
        block_bias = jnp.concatenate([bias[:keys, rows]] * GROUP, axis=1)
        scores = dot_nt(key[:keys], query) * (score_scale * LOG2E) + block_bias
        weights = jnp.exp2(scores - jnp.max(scores, axis=0, keepdims=True))
        probs = weights * (1.0 / jnp.sum(weights, axis=0, keepdims=True))
        prob_grad = dot_nt(value[:keys], grad)
        delta = jnp.sum(probs * prob_grad, axis=0, keepdims=True)
        score_grad = (probs * (prob_grad - delta)).astype(BF)
        sums.append((dot(score_grad, query), dot(probs.astype(BF), grad)))
    key_rot = jnp.concatenate([sums[0][0] + sums[1][0][:half], sums[1][0][half:]], axis=0)
    value_grad = jnp.concatenate([sums[0][1] + sums[1][1][:half], sums[1][1][half:]], axis=0)
    key_rot = key_rot * score_scale
    swapped = jnp.concatenate([key_rot[:, HEAD // 2 :], key_rot[:, : HEAD // 2]], axis=1)
    key_grad = key_rot * cos[...] + swapped * sin[...]

    key_grad = key_grad.astype(BF)
    value_grad = value_grad.astype(BF)
    grad_out[:, pl.ds(pl.multiple_of((step * STEP_HEADS + i) * HEAD, HEAD), HEAD)] = key_grad
    grad_out[:, pl.ds(
        pl.multiple_of(KEY_HEAD_WIDTH + (step * STEP_HEADS + i) * HEAD, HEAD), HEAD
    )] = value_grad
    up_rows = up[:, part]
    zero = jnp.zeros((ADAPTER_RANK, HEAD), BF)
    key_up = jnp.concatenate([up_rows[:ADAPTER_RANK], zero], axis=0)
    value_up = jnp.concatenate([zero, up_rows[ADAPTER_RANK:]], axis=0)
    lift[...] += dot_nt(
        jnp.concatenate([key_grad, value_grad], axis=1),
        jnp.concatenate([key_up, value_up], axis=1),
    )


def attention_kernel(
    pick_row, seg_row, cos, sin, up, q, g, k, v, near, far, grad_out, lift_out,
    gather, bias, lift, spread, spread_far
):
    step = pl.program_id(0)

    @pl.when(step == 0)
    def _():
        gather[...] = arrival_pick(to_column(pick_row[...]), iota((ROWS, ARRIVALS), 1))
        allowed = (to_column(seg_row[...]) == seg_row[...]) & (
            iota((ROWS, ROWS), 0) <= iota((ROWS, ROWS), 1)
        )
        bias[...] = jnp.where(allowed, 0.0, -1e30)
        lift[...] = jnp.zeros_like(lift)

    for i in range(STEP_HEADS):
        head_grads(step, i, up, q, g, k, v, near, far, grad_out, gather, bias, lift, spread, spread_far, cos, sin)

    @pl.when(step == KV_HEADS // STEP_HEADS - 1)
    def _():
        lift_out[...] = lift[...].astype(BF)


def attention(pick_row, seg_row, cos, sin, up, queries, grads, kv, near, far):
    def whole(shape):
        return pl.BlockSpec(shape, lambda j: (0,) * len(shape))

    def head_block(width):
        return pl.BlockSpec((ROWS, width), lambda j: (0, j))

    arrived = pl.BlockSpec((PEERS, 16, STEP_HEADS * HEAD_QUARTER), lambda j: (0, 0, j))
    return pl.pallas_call(
        attention_kernel,
        grid=(KV_HEADS // STEP_HEADS,),
        in_specs=[
            whole((1, ROWS)),
            whole((1, ROWS)),
            whole((ROWS, HEAD)),
            whole((ROWS, HEAD)),
            pl.BlockSpec((2 * ADAPTER_RANK, STEP_HEADS * HEAD), lambda j: (0, j)),
            head_block(STEP_HEADS * GROUP_WIDTH),
            head_block(STEP_HEADS * GROUP_WIDTH),
            head_block(STEP_HEADS * HEAD),
            pl.BlockSpec((ROWS, STEP_HEADS * HEAD), lambda j: (0, KV_HEADS // STEP_HEADS + j)),
            arrived,
            arrived,
        ],
        out_specs=[whole((ROWS, 2 * KEY_HEAD_WIDTH)), whole((ROWS, HEAD))],
        out_shape=[
            jax.ShapeDtypeStruct((ROWS, 2 * KEY_HEAD_WIDTH), BF),
            jax.ShapeDtypeStruct((ROWS, HEAD), BF),
        ],
        scratch_shapes=[
            pltpu.VMEM((ROWS, ARRIVALS), BF),
            pltpu.VMEM((ROWS, ROWS), F32),
            pltpu.VMEM((ROWS, HEAD), F32),
            pltpu.VMEM((STEP_HEADS, HEAD_QUARTER // HEAD, ROWS, HEAD), F32),
            pltpu.VMEM((STEP_HEADS, HEAD_QUARTER // HEAD, ROWS, HEAD), F32),
        ],
        compiler_params=pltpu.CompilerParams(vmem_limit_bytes=VMEM_LIMIT),
        cost_estimate=pl.CostEstimate(
            flops=12 * 10**9, bytes_accessed=14 * MIB, transcendentals=2 * 10**6
        ),
        name="attention_grads",
    )(pick_row, seg_row, cos, sin, up, queries, grads, kv, kv, near, far)


def adapter_kernel(
    pick_row, first_core, core_step, lift, own_down, near_down, near_x, far, x, kv_grad,
    keep, give, x_in, kv_in, far_in, near_in, placed_out, spread, load_sem, out_sem
):
    loads = [
        pltpu.make_async_copy(far, far_in, load_sem.at[0]),
        pltpu.make_async_copy(kv_grad, kv_in, load_sem.at[1]),
        pltpu.make_async_copy(near_x, near_in, load_sem.at[2]),
    ]
    for c in range(QUARTERS):
        part = columns(c, X_QUARTER)
        loads.append(pltpu.make_async_copy(x.at[:, part], x_in.at[:, part], load_sem.at[3 + c]))
    for load in loads:
        load.start()

    core = lax.rem(lax.axis_index("local"), 2)
    column = iota((PART_ROWS, PART_COLS), 1)
    orders = [
        jnp.concatenate(
            [
                jnp.where(
                    column == first_core[...] + (at * core_step[...] + k * PART_SHIFT), 1.0, 0.0
                ).astype(BF)
                for at in (core, 1 - core)
            ],
            axis=0,
        )
        for k in range(PARTS)
    ]
    gather = arrival_pick(to_column(pick_row[...]), iota((ROWS, ARRIVALS), 1))
    spread_lift = arrival_pick(pick_row[...], iota((ARRIVALS, ROWS), 0))
    lifted = dot(spread_lift, lift[...]).astype(BF)

    loads[0].wait()
    far_rows = gather_quarters(far_in[:, :, :X_QUARTER], spread)
    spread[0] = far_in[:, :, X_QUARTER:].reshape(ROWS, HEAD).astype(F32)
    far_down = spread[0, pl.ds(0, MOVED, stride=QUARTERS), :].astype(BF)

    arrived_down = jnp.concatenate([own_down[...], near_down[...], far_down], axis=0)
    down_out = dot(gather, arrived_down).astype(BF)
    loads[1].wait()
    up_both = dot_tn(down_out, kv_in[...])
    up_sum = jnp.concatenate(
        [up_both[:ADAPTER_RANK, :KEY_HEAD_WIDTH], up_both[ADAPTER_RANK:, KEY_HEAD_WIDTH:]], axis=0
    ).astype(BF)

    loads[2].wait()
    stores = []
    for z_lo in range(BLOCK_COUNT // 2):
        part = columns(z_lo, X_QUARTER)
        loads[3 + z_lo].wait()
        arrived = jnp.concatenate([x_in[:, part], near_in[:, part], far_rows[:, part]], axis=0)
        down_sum = dot_tn(lifted, arrived).astype(BF)
        rows = columns(z_lo, 2 * SHARD)
        for k in range(PARTS):
            y_low, x_high = k // 2, k % 2
            both = []
            for y_high in range(2):
                start = y_high * DOWN_BLOCK + k * HEAD
                both.append(
                    jnp.concatenate(
                        [
                            down_sum[:, start : start + 2 * HEAD],
                            up_sum[:, columns(2 * z_lo + y_high, UP_BLOCK)],
                        ],
                        axis=1,
                    )
                )
            placed = dot_nt(orders[k], jnp.concatenate(both, axis=0)).astype(BF)
            for c in range(2):
                for x_low in range(2):
                    at = (c * 2 + x_low) * 2 * SHARD
                    for y_high in range(2):
                        y = y_high * 2 + y_low
                        placed_out[c, (x_high * 2 + x_low) * 4 + y, rows, :] = placed[
                            at : at + 2 * SHARD, columns(y_high, HEAD)
                        ]
        for c, out in enumerate((give, keep)):
            stores.append(
                pltpu.make_async_copy(
                    placed_out.at[1 - c, :, rows], out.at[:, rows], out_sem.at[2 * z_lo + c]
                )
            )
            stores[-1].start()
    for store in stores:
        store.wait()


def shard_order():
    order, step = [], []
    for x_low in range(2):
        for z_hi in range(2):
            device = (x_low * 2 + z_hi) * 2
            order += [device * DOWN_SHARD + r for r in range(DOWN_SHARD)]
            order += [2 * HEAD + device * UP_SHARD + r for r in range(UP_SHARD)]
            step += [DOWN_SHARD] * DOWN_SHARD + [UP_SHARD] * UP_SHARD
    return [np.asarray(a, np.int32).reshape(PART_ROWS, 1) for a in (order, step)]


def adapters(pick_row, lift, own_down, near_down, near_x, far, x, kv_grad):
    hbm, vmem = pl.BlockSpec(memory_space=pltpu.HBM), pl.BlockSpec(memory_space=pltpu.VMEM)
    first_core, core_step = [jnp.asarray(a) for a in shard_order()]
    half = jax.ShapeDtypeStruct((16, 8 * SHARD, HEAD), BF)
    return pl.pallas_call(
        adapter_kernel,
        out_shape=[half, half],
        in_specs=[vmem] * 6 + [hbm] * 4,
        out_specs=[hbm, hbm],
        scratch_shapes=[
            pltpu.VMEM((ROWS, MODEL_WIDTH), BF),
            pltpu.VMEM((ROWS, 2 * KEY_HEAD_WIDTH), BF),
            pltpu.VMEM((PEERS, 16, X_QUARTER + HEAD), BF),
            pltpu.VMEM((MOVED, MODEL_WIDTH), BF),
            pltpu.VMEM((2, 16, 8 * SHARD, HEAD), BF),
            pltpu.VMEM((X_QUARTER // HEAD, ROWS, HEAD), F32),
            pltpu.SemaphoreType.DMA((3 + QUARTERS,)),
            pltpu.SemaphoreType.DMA((BLOCK_COUNT,)),
        ],
        compiler_params=pltpu.CompilerParams(vmem_limit_bytes=VMEM_LIMIT),
        cost_estimate=pl.CostEstimate(
            flops=4 * 10**9, bytes_accessed=10 * MIB, transcendentals=0
        ),
        name="adapter_grads",
    )(
        pick_row,
        first_core,
        core_step,
        lift,
        own_down,
        near_down,
        near_x,
        far,
        x,
        kv_grad,
    )


def device_groups(axes):
    names = ["z_lo", "y", "x", "z_hi", "core"]
    index = np.arange(256).reshape(4, 4, 4, 2, 2)
    moved = [names.index(a) for a in axes]
    rest = [i for i in range(5) if i not in moved]
    size = math.prod(index.shape[i] for i in moved)
    return index.transpose(rest + moved).reshape(-1, size).tolist()


def exchange(array, axes):
    return lax.all_to_all(
        array,
        ("node", "local"),
        split_axis=0,
        concat_axis=0,
        axis_index_groups=device_groups(axes),
        tiled=True,
    )


def sum_over_devices(keep, give):
    got = lax.ppermute(give, ("node", "local"), [(i, i ^ 1) for i in range(256)])
    total = (keep.astype(F32) + got.astype(F32)).astype(BF)
    total = jnp.sum(exchange(total, ["x", "y"]).astype(F32), axis=0)
    total = total.reshape(8, SHARD, HEAD)
    return jnp.sum(exchange(total, ["z_lo", "z_hi"]), axis=0)


def rope_tables(segments):
    slot_ids = jnp.arange(segments.shape[0], dtype=jnp.int32)
    seg_start = jnp.sum((segments[None, :] < segments[:, None]).astype(jnp.int32), axis=1)
    position = (slot_ids - seg_start).astype(F32)
    frequency = ROPE_THETA ** (-jnp.arange(0, HEAD, 2).astype(F32) / HEAD)
    angles = position[:, None] * frequency[None, :]
    cosine, sine = jnp.cos(angles), jnp.sin(angles)
    return (
        jnp.concatenate([cosine, cosine], axis=1),
        jnp.concatenate([sine, -sine], axis=1),
    )


def local(
    activations,
    queries,
    rotated_key_value,
    attention_out_grad,
    adapter_down,
    adapter_up,
    bin_local_index,
    bin_row_offset,
    spill_node,
    spill_row_offset,
    arrival_pick_index,
    packed_sequence_number,
):
    plan = (bin_local_index, bin_row_offset, spill_node, spill_row_offset)
    rows = (queries, attention_out_grad, rotated_key_value, activations)
    (near_send,) = pack(plan, *rows)
    far_send, far_x_send, own_down = pack(plan, *rows, adapter_down)

    near = lax.all_to_all(near_send, "local", split_axis=0, concat_axis=0, tiled=True)
    far_send, near = lax.optimization_barrier((far_send, near))
    far = lax.all_to_all(far_send, "node", split_axis=0, concat_axis=0, tiled=True)
    near_x, near_down = near_adapter_rows(near[:, :, ATT_COLS:], adapter_down)
    pick_row = arrival_pick_index
    seg_row = packed_sequence_number
    cos, sin = rope_tables(packed_sequence_number.reshape(-1))
    far_x_send, far, near_x, near_down, cos, sin = lax.optimization_barrier(
        (far_x_send, far, near_x, near_down, cos, sin)
    )
    far_x = lax.all_to_all(far_x_send, "node", split_axis=0, concat_axis=0, tiled=True)

    kv_grad, lift = attention(
        pick_row,
        seg_row,
        cos,
        sin,
        adapter_up,
        queries,
        attention_out_grad,
        rotated_key_value,
        near,
        far,
    )
    keep, give = adapters(
        pick_row,
        lift,
        own_down,
        near_down,
        near_x,
        far_x,
        activations,
        kv_grad,
    )
    total = sum_over_devices(keep, give) * (1.0 / math.sqrt(256 * ROWS))
    return (kv_grad, total[:DOWN_SHARD], total[DOWN_SHARD:])


def solution(mesh):
    split = P(("node", "local"), None)
    return jax.shard_map(
        local,
        mesh=mesh,
        in_specs=(split,) * 4 + (P(), P()) + (split,) * 6,
        out_specs=(split,) * 3,
        check_vma=False,
    )
```

```python
import functools
import math

import numpy as np

import jax
import jax.numpy as jnp
from jax import lax
from jax.experimental import pallas as pl
from jax.experimental.pallas import tpu as pltpu
from jax.sharding import PartitionSpec as P

KV_HEADS = 8
HEAD = 128
ADAPTER_RANK = 64
CAP_L = 4
CAP_N = 4
GROUP = 5
KEY_HEAD_WIDTH = 1024
MODEL_WIDTH = 5120
ROWS = 256
PEERS = 16
MOVED = PEERS * CAP_L
ARRIVALS = ROWS + 2 * MOVED
ROPE_THETA = 1000000.0

QUARTERS = 4
GROUP_WIDTH = GROUP * HEAD
HEAD_COLS = 2 * GROUP_WIDTH + 2 * HEAD
HEAD_QUARTER = HEAD_COLS // QUARTERS
ATT_COLS = KV_HEADS * HEAD_QUARTER
X_QUARTER = MODEL_WIDTH // QUARTERS
LOG2E = math.log2(math.e)
BF = jnp.bfloat16
F32 = jnp.float32
MIB = 1 << 20
VMEM_LIMIT = 62 * MIB

DOWN_SHARD = 20
UP_SHARD = 4
SHARD = DOWN_SHARD + UP_SHARD
BLOCK_DEV = 32
BLOCK_COUNT = 8
DOWN_BLOCK = BLOCK_DEV * DOWN_SHARD
UP_BLOCK = BLOCK_DEV * UP_SHARD
PARTS = 4
PART_ROWS = 4 * SHARD
PART_COLS = 3 * HEAD
PART_SHIFT = 32


def dot(a, b):
    return jnp.dot(a, b, preferred_element_type=F32)


def dot_nt(a, b):
    return lax.dot_general(a, b, (((1,), (1,)), ((), ())), preferred_element_type=F32)


def dot_tn(a, b):
    return lax.dot_general(a, b, (((0,), (0,)), ((), ())), preferred_element_type=F32)


def iota(shape, dim):
    return lax.broadcasted_iota(jnp.int32, shape, dim)


def interleave(rows, scratch):
    blocks = scratch.shape[0]
    for c in range(QUARTERS):
        for i in range(blocks):
            at = (c * blocks + i) * HEAD
            scratch[i, pl.ds(c, MOVED, stride=QUARTERS), :] = rows[:, at : at + HEAD]
    wide = jnp.concatenate([scratch[i] for i in range(blocks)], axis=1)
    return wide.astype(BF).reshape(PEERS, 16, blocks * HEAD)


def gather_quarters(rows, scratch):
    blocks = scratch.shape[0]
    wide = rows.reshape(ROWS, blocks * HEAD).astype(F32)
    for i in range(blocks):
        scratch[i] = wide[:, i * HEAD : (i + 1) * HEAD]
    return jnp.concatenate(
        [
            scratch[i, pl.ds(c, MOVED, stride=QUARTERS), :]
            for c in range(QUARTERS)
            for i in range(blocks)
        ],
        axis=1,
    ).astype(BF)


X_STEPS = 5
X_STEP = X_QUARTER // X_STEPS


def columns(j, width):
    return slice(j * width, (j + 1) * width)


def pack_kernel(near, bin_local, bin_offset, spill_node, spill_offset, q, g, kv, x, *rest):
    if near:
        att_out, *rest = rest
        x_out, x_from = att_out, ATT_COLS
    else:
        down, att_out, x_out, *rest = rest
        x_from = 0
    q_in, g_in, kv_in, x_in, att, att_x, spread, spread_x, head_sem, x_sem, out_sem, *rest = rest

    loads = [pltpu.make_async_copy(kv, kv_in, head_sem.at[2 * KV_HEADS])]
    for j in range(KV_HEADS):
        part = columns(j, GROUP_WIDTH)
        loads.append(pltpu.make_async_copy(q.at[:, part], q_in.at[:, part], head_sem.at[2 * j]))
        loads.append(
            pltpu.make_async_copy(g.at[:, part], g_in.at[:, part], head_sem.at[2 * j + 1])
        )
    x_loads = []
    for c in range(QUARTERS):
        part = columns(c, X_QUARTER)
        x_loads.append(pltpu.make_async_copy(x.at[:, part], x_in.at[:, part], x_sem.at[c]))
    if not near:
        down_in, att_down, down_sem = rest
        x_loads.append(pltpu.make_async_copy(down, down_in, down_sem.at[0]))
    for load in loads + x_loads:
        load.start()

    stays_in = bin_local[...] == lax.axis_index("local")
    if near:
        target = jnp.where(stays_in, -1, bin_local[...] * CAP_L + bin_offset[...])
    else:
        moves = stays_in & (spill_node[...] != lax.axis_index("node"))
        target = jnp.where(moves, spill_node[...] * CAP_N + spill_offset[...], -1)
    select = jnp.where(iota((MOVED, ROWS), 0) == target, 1.0, 0.0).astype(BF)
    stores = []

    def send(source, to, sem):
        stores.append(pltpu.make_async_copy(source, to, sem))
        stores[-1].start()

    loads[0].wait()
    for j in range(KV_HEADS):
        loads[1 + 2 * j].wait()
        loads[2 + 2 * j].wait()
        part = columns(j, GROUP_WIDTH)
        rows = jnp.concatenate(
            [
                q_in[:, part],
                g_in[:, part],
                kv_in[:, columns(j, HEAD)],
                kv_in[:, columns(KV_HEADS + j, HEAD)],
            ],
            axis=1,
        )
        part = columns(j, HEAD_QUARTER)
        att[:, :, part] = interleave(dot(select, rows), spread.at[j % 2])
        send(att.at[:, :, part], att_out.at[:, :, part], out_sem.at[j])
    for load in x_loads:
        load.wait()
    moved_down = 0.0
    for j in range(X_STEPS):
        rows = jnp.concatenate(
            [x_in[:, columns(c * X_STEPS + j, X_STEP)] for c in range(QUARTERS)], axis=1
        )
        part = columns(j, X_STEP)
        picked = dot(select, rows)
        att_x[:, :, part] = interleave(picked, spread_x.at[j % 2])
        if not near:
            down_rows = jnp.concatenate(
                [down_in[columns(c * X_STEPS + j, X_STEP)] for c in range(QUARTERS)], axis=0
            )
            moved_down = moved_down + dot(picked.astype(BF), down_rows)
        to = slice(x_from + part.start, x_from + part.stop)
        send(att_x.at[:, :, part], x_out.at[:, :, to], out_sem.at[KV_HEADS + j])
    if not near:
        picked = moved_down.astype(BF).astype(F32)
        rows = jnp.concatenate([picked] + [jnp.zeros_like(picked)] * (QUARTERS - 1), axis=1)
        att_down[...] = interleave(rows, spread_x.at[0, :1])
        send(att_down, x_out.at[:, :, X_QUARTER:], down_sem.at[1])
    for store in stores:
        store.wait()


def pack(plan, queries, grads, kv, activations, down=None):
    near = down is None
    hbm, vmem = pl.BlockSpec(memory_space=pltpu.HBM), pl.BlockSpec(memory_space=pltpu.VMEM)
    scratch = [
        pltpu.VMEM((ROWS, KV_HEADS * GROUP_WIDTH), BF),
        pltpu.VMEM((ROWS, KV_HEADS * GROUP_WIDTH), BF),
        pltpu.VMEM((ROWS, 2 * KEY_HEAD_WIDTH), BF),
        pltpu.VMEM((ROWS, MODEL_WIDTH), BF),
        pltpu.VMEM((PEERS, 16, ATT_COLS), BF),
        pltpu.VMEM((PEERS, 16, X_QUARTER), BF),
        pltpu.VMEM((2, HEAD_QUARTER // HEAD, ROWS, HEAD), F32),
        pltpu.VMEM((2, X_STEP // HEAD, ROWS, HEAD), F32),
        pltpu.SemaphoreType.DMA((2 * KV_HEADS + 1,)),
        pltpu.SemaphoreType.DMA((QUARTERS,)),
        pltpu.SemaphoreType.DMA((KV_HEADS + X_STEPS,)),
    ]
    if near:
        args, out_specs = (), [hbm]
        out_shape = [jax.ShapeDtypeStruct((PEERS, 16, ATT_COLS + X_QUARTER), BF)]
    else:
        args, out_specs = (down,), [hbm, hbm]
        out_shape = [
            jax.ShapeDtypeStruct((PEERS, 16, ATT_COLS), BF),
            jax.ShapeDtypeStruct((PEERS, 16, X_QUARTER + HEAD), BF),
        ]
        scratch += [
            pltpu.VMEM((MODEL_WIDTH, HEAD), BF),
            pltpu.VMEM((PEERS, 16, HEAD), BF),
            pltpu.SemaphoreType.DMA((2,)),
        ]
    return pl.pallas_call(
        functools.partial(pack_kernel, near),
        in_specs=[vmem] * 4 + [hbm] * (4 + len(args)),
        out_specs=out_specs,
        out_shape=out_shape,
        scratch_shapes=scratch,
        compiler_params=pltpu.CompilerParams(vmem_limit_bytes=VMEM_LIMIT),
        cost_estimate=pl.CostEstimate(
            flops=2 * MOVED * ROWS * QUARTERS * (ATT_COLS + X_QUARTER),
            bytes_accessed=14 * MIB,
            transcendentals=0,
        ),
        name="pack_rows",
    )(*plan, queries, grads, kv, activations, *args)


def near_kernel(near, x, down, near_x_out, down_out, spread):
    rows = gather_quarters(near[...], spread)
    near_x_out[...] = rows
    down_out[:ROWS] = dot(x[...], down[...]).astype(BF)
    down_out[ROWS:] = dot(rows, down[...]).astype(BF)


def near_adapter_rows(near, x, down):
    def whole(*shape):
        return pl.BlockSpec(shape, lambda i: (0,) * len(shape))

    return pl.pallas_call(
        near_kernel,
        grid=(1,),
        in_specs=[
            whole(PEERS, 16, X_QUARTER),
            whole(ROWS, MODEL_WIDTH),
            whole(MODEL_WIDTH, HEAD),
        ],
        out_specs=[whole(MOVED, MODEL_WIDTH), whole(ROWS + MOVED, HEAD)],
        out_shape=[
            jax.ShapeDtypeStruct((MOVED, 40 * MODEL_WIDTH), BF),
            jax.ShapeDtypeStruct((ROWS + MOVED, HEAD), BF),
        ],
        scratch_shapes=[pltpu.VMEM((X_QUARTER // HEAD, ROWS, HEAD), F32)],
        compiler_params=pltpu.CompilerParams(vmem_limit_bytes=32 * MIB),
        cost_estimate=pl.CostEstimate(
            flops=2 * MOVED * MODEL_WIDTH * HEAD, bytes_accessed=9 * MIB, transcendentals=0
        ),
        name="near_adapter_rows",
    )(near, x, down)


def to_column(row):
    diagonal = iota((ROWS, ROWS), 0) == iota((ROWS, ROWS), 1)
    return jnp.sum(jnp.where(diagonal, row, 0), axis=1, keepdims=True)


def arrival_pick(pick, entry):
    return jnp.where(pick == entry, 1.0, 0.0).astype(BF)


STEP_HEADS = 2


def head_grads(
    step, i, up, q, g, k, v, near, far, grad_out, gather, bias, lift, spread, spread_far, cos, sin
):
    part, wide = columns(i, HEAD), columns(i, GROUP_WIDTH)
    own_rows = jnp.concatenate([q[:, wide], g[:, wide], k[:, part], v[:, part]], axis=1)
    near_rows = gather_quarters(near[:, :, columns(i, HEAD_QUARTER)], spread.at[i])
    far_rows = gather_quarters(far[:, :, columns(i, HEAD_QUARTER)], spread_far.at[i])
    packed = dot(gather[...], jnp.concatenate([own_rows, near_rows, far_rows], axis=0)).astype(BF)
    key = packed[:, 2 * GROUP_WIDTH : 2 * GROUP_WIDTH + HEAD]
    value = packed[:, 2 * GROUP_WIDTH + HEAD :]
    score_scale = 1.0 / math.sqrt(HEAD)

    half = ROWS // 2
    sums = []
    for block in range(2):
        rows = slice(block * half, (block + 1) * half)
        keys = (block + 1) * half
        query = jnp.concatenate(
            [packed[rows, h * HEAD : (h + 1) * HEAD] for h in range(GROUP)], axis=0
        )
        grad = jnp.concatenate(
            [packed[rows, GROUP_WIDTH + h * HEAD : GROUP_WIDTH + (h + 1) * HEAD] for h in range(GROUP)],
            axis=0,
        )
        block_bias = jnp.concatenate([bias[:keys, rows]] * GROUP, axis=1)
        scores = dot_nt(key[:keys], query) * (score_scale * LOG2E) + block_bias
        weights = jnp.exp2(scores - jnp.max(scores, axis=0, keepdims=True))
        probs = weights * (1.0 / jnp.sum(weights, axis=0, keepdims=True))
        prob_grad = dot_nt(value[:keys], grad)
        delta = jnp.sum(probs * prob_grad, axis=0, keepdims=True)
        score_grad = (probs * (prob_grad - delta)).astype(BF)
        sums.append((dot(score_grad, query), dot(probs.astype(BF), grad)))
    key_rot = jnp.concatenate([sums[0][0] + sums[1][0][:half], sums[1][0][half:]], axis=0)
    value_grad = jnp.concatenate([sums[0][1] + sums[1][1][:half], sums[1][1][half:]], axis=0)
    key_rot = key_rot * score_scale
    swapped = jnp.concatenate([key_rot[:, HEAD // 2 :], key_rot[:, : HEAD // 2]], axis=1)
    key_grad = key_rot * cos[...] + swapped * sin[...]

    key_grad = key_grad.astype(BF)
    value_grad = value_grad.astype(BF)
    grad_out[:, pl.ds(pl.multiple_of((step * STEP_HEADS + i) * HEAD, HEAD), HEAD)] = key_grad
    grad_out[:, pl.ds(
        pl.multiple_of(KEY_HEAD_WIDTH + (step * STEP_HEADS + i) * HEAD, HEAD), HEAD
    )] = value_grad
    up_rows = up[:, part]
    zero = jnp.zeros((ADAPTER_RANK, HEAD), BF)
    key_up = jnp.concatenate([up_rows[:ADAPTER_RANK], zero], axis=0)
    value_up = jnp.concatenate([zero, up_rows[ADAPTER_RANK:]], axis=0)
    lift[...] += dot_nt(
        jnp.concatenate([key_grad, value_grad], axis=1),
        jnp.concatenate([key_up, value_up], axis=1),
    )


def attention_kernel(
    pick_row, seg_row, cos, sin, up, q, g, k, v, near, far, grad_out, lift_out,
    gather, bias, lift, spread, spread_far
):
    step = pl.program_id(0)

    @pl.when(step == 0)
    def _():
        gather[...] = arrival_pick(to_column(pick_row[...]), iota((ROWS, ARRIVALS), 1))
        allowed = (to_column(seg_row[...]) == seg_row[...]) & (
            iota((ROWS, ROWS), 0) <= iota((ROWS, ROWS), 1)
        )
        bias[...] = jnp.where(allowed, 0.0, -1e30)
        lift[...] = jnp.zeros_like(lift)

    for i in range(STEP_HEADS):
        head_grads(step, i, up, q, g, k, v, near, far, grad_out, gather, bias, lift, spread, spread_far, cos, sin)

    @pl.when(step == KV_HEADS // STEP_HEADS - 1)
    def _():
        lift_out[...] = lift[...].astype(BF)


def attention(pick_row, seg_row, cos, sin, up, queries, grads, kv, near, far):
    def whole(shape):
        return pl.BlockSpec(shape, lambda j: (0,) * len(shape))

    def head_block(width):
        return pl.BlockSpec((ROWS, width), lambda j: (0, j))

    arrived = pl.BlockSpec((PEERS, 16, STEP_HEADS * HEAD_QUARTER), lambda j: (0, 0, j))
    return pl.pallas_call(
        attention_kernel,
        grid=(KV_HEADS // STEP_HEADS,),
        in_specs=[
            whole((1, ROWS)),
            whole((1, ROWS)),
            whole((ROWS, HEAD)),
            whole((ROWS, HEAD)),
            pl.BlockSpec((2 * ADAPTER_RANK, STEP_HEADS * HEAD), lambda j: (0, j)),
            head_block(STEP_HEADS * GROUP_WIDTH),
            head_block(STEP_HEADS * GROUP_WIDTH),
            head_block(STEP_HEADS * HEAD),
            pl.BlockSpec((ROWS, STEP_HEADS * HEAD), lambda j: (0, KV_HEADS // STEP_HEADS + j)),
            arrived,
            arrived,
        ],
        out_specs=[whole((ROWS, 2 * KEY_HEAD_WIDTH)), whole((ROWS, HEAD))],
        out_shape=[
            jax.ShapeDtypeStruct((ROWS, 2 * KEY_HEAD_WIDTH), BF),
            jax.ShapeDtypeStruct((ROWS, 384 * HEAD), BF),
        ],
        scratch_shapes=[
            pltpu.VMEM((ROWS, ARRIVALS), BF),
            pltpu.VMEM((ROWS, ROWS), F32),
            pltpu.VMEM((ROWS, HEAD), F32),
            pltpu.VMEM((STEP_HEADS, HEAD_QUARTER // HEAD, ROWS, HEAD), F32),
            pltpu.VMEM((STEP_HEADS, HEAD_QUARTER // HEAD, ROWS, HEAD), F32),
        ],
        compiler_params=pltpu.CompilerParams(vmem_limit_bytes=54 * MIB),
        cost_estimate=pl.CostEstimate(
            flops=12 * 10**9, bytes_accessed=14 * MIB, transcendentals=2 * 10**6
        ),
        name="attention_grads",
    )(pick_row, seg_row, cos, sin, up, queries, grads, kv, kv, near, far)


def adapter_kernel(
    pick_row, first_core, core_step, near_down, x, far, lift, near_x, kv_grad,
    keep, give, _kv_grad, lift_in, near_in, kv_in, far_in, placed_out, spread, load_sem, out_sem
):
    loads = [
        pltpu.make_async_copy(source, to, load_sem.at[i])
        for i, (source, to) in enumerate(
            (
                (lift.at[:, :HEAD], lift_in),
                (far, far_in),
                (kv_grad, kv_in),
                (near_x.at[:, :MODEL_WIDTH], near_in),
            )
        )
    ]
    for load in loads:
        load.start()

    core = lax.rem(lax.axis_index("local"), 2)
    column = iota((PART_ROWS, PART_COLS), 1)
    orders = [
        jnp.concatenate(
            [
                jnp.where(
                    column == first_core[...] + (at * core_step[...] + k * PART_SHIFT), 1.0, 0.0
                ).astype(BF)
                for at in (core, 1 - core)
            ],
            axis=0,
        )
        for k in range(PARTS)
    ]
    gather = arrival_pick(to_column(pick_row[...]), iota((ROWS, ARRIVALS), 1))
    spread_lift = arrival_pick(pick_row[...], iota((ARRIVALS, ROWS), 0))
    loads[0].wait()
    lifted = dot(spread_lift, lift_in[...]).astype(BF)

    loads[1].wait()
    far_rows = gather_quarters(far_in[:, :, :X_QUARTER], spread)
    spread[0] = far_in[:, :, X_QUARTER:].reshape(ROWS, HEAD).astype(F32)
    far_down = spread[0, pl.ds(0, MOVED, stride=QUARTERS), :].astype(BF)

    arrived_down = jnp.concatenate([near_down[...], far_down], axis=0)
    down_out = dot(gather, arrived_down).astype(BF)
    loads[2].wait()
    up_both = dot_tn(down_out, kv_in[...])
    up_sum = jnp.concatenate(
        [up_both[:ADAPTER_RANK, :KEY_HEAD_WIDTH], up_both[ADAPTER_RANK:, KEY_HEAD_WIDTH:]], axis=0
    ).astype(BF)

    loads[3].wait()
    stores = []
    for z_lo in range(BLOCK_COUNT // 2):
        part = columns(z_lo, X_QUARTER)
        arrived = jnp.concatenate([x[:, part], near_in[:, part], far_rows[:, part]], axis=0)
        down_sum = dot_tn(lifted, arrived).astype(BF)
        rows = columns(z_lo, 2 * SHARD)
        for k in range(PARTS):
            y_low, x_high = k // 2, k % 2
            both = []
            for y_high in range(2):
                start = y_high * DOWN_BLOCK + k * HEAD
                both.append(
                    jnp.concatenate(
                        [
                            down_sum[:, start : start + 2 * HEAD],
                            up_sum[:, columns(2 * z_lo + y_high, UP_BLOCK)],
                        ],
                        axis=1,
                    )
                )
            placed = dot_nt(orders[k], jnp.concatenate(both, axis=0)).astype(BF)
            for c in range(2):
                for x_low in range(2):
                    at = (c * 2 + x_low) * 2 * SHARD
                    for y_high in range(2):
                        y = y_high * 2 + y_low
                        placed_out[c, (x_high * 2 + x_low) * 4 + y, rows, :] = placed[
                            at : at + 2 * SHARD, columns(y_high, HEAD)
                        ]
        for c, out in enumerate((give, keep)):
            stores.append(
                pltpu.make_async_copy(
                    placed_out.at[1 - c, :, rows], out.at[:, rows], out_sem.at[2 * z_lo + c]
                )
            )
            stores[-1].start()
    for store in stores:
        store.wait()


def shard_order():
    order, step = [], []
    for x_low in range(2):
        for z_hi in range(2):
            device = (x_low * 2 + z_hi) * 2
            order += [device * DOWN_SHARD + r for r in range(DOWN_SHARD)]
            order += [2 * HEAD + device * UP_SHARD + r for r in range(UP_SHARD)]
            step += [DOWN_SHARD] * DOWN_SHARD + [UP_SHARD] * UP_SHARD
    return [np.asarray(a, np.int32).reshape(PART_ROWS, 1) for a in (order, step)]


def adapters(pick_row, near_down, x, far, lift, near_x, kv_grad):
    hbm, vmem = pl.BlockSpec(memory_space=pltpu.HBM), pl.BlockSpec(memory_space=pltpu.VMEM)
    place = pl.BlockSpec(memory_space=pl.ANY)
    first_core, core_step = [jnp.asarray(a) for a in shard_order()]
    half = jax.ShapeDtypeStruct((16, 8 * SHARD, HEAD), BF)
    passed = jax.ShapeDtypeStruct(kv_grad.shape, kv_grad.dtype)
    return pl.pallas_call(
        adapter_kernel,
        out_shape=[half, half, passed],
        input_output_aliases={8: 2},
        in_specs=[vmem] * 5 + [hbm] * 4,
        out_specs=[place, place, hbm],
        scratch_shapes=[
            pltpu.VMEM((ROWS, HEAD), BF),
            pltpu.VMEM((MOVED, MODEL_WIDTH), BF),
            pltpu.VMEM((ROWS, 2 * KEY_HEAD_WIDTH), BF),
            pltpu.VMEM((PEERS, 16, X_QUARTER + HEAD), BF),
            pltpu.VMEM((2, 16, 8 * SHARD, HEAD), BF),
            pltpu.VMEM((X_QUARTER // HEAD, ROWS, HEAD), F32),
            pltpu.SemaphoreType.DMA((4,)),
            pltpu.SemaphoreType.DMA((BLOCK_COUNT,)),
        ],
        compiler_params=pltpu.CompilerParams(vmem_limit_bytes=40 * MIB),
        cost_estimate=pl.CostEstimate(
            flops=4 * 10**9, bytes_accessed=10 * MIB, transcendentals=0
        ),
        name="adapter_grads",
    )(pick_row, first_core, core_step, near_down, x, far, lift, near_x, kv_grad)


def device_groups(axes):
    names = ["z_lo", "y", "x", "z_hi", "core"]
    index = np.arange(256).reshape(4, 4, 4, 2, 2)
    moved = [names.index(a) for a in axes]
    rest = [i for i in range(5) if i not in moved]
    size = math.prod(index.shape[i] for i in moved)
    return index.transpose(rest + moved).reshape(-1, size).tolist()


def exchange(array, axes):
    return lax.all_to_all(
        array,
        ("node", "local"),
        split_axis=0,
        concat_axis=0,
        axis_index_groups=device_groups(axes),
        tiled=True,
    )


def sum_over_devices(keep, give):
    got = lax.ppermute(give, ("node", "local"), [(i, i ^ 1) for i in range(256)])
    total = (keep.astype(F32) + got.astype(F32)).astype(BF)
    total = jnp.sum(exchange(total, ["x", "y"]).astype(F32), axis=0)
    total = total.reshape(8, SHARD, HEAD)
    return jnp.sum(exchange(total, ["z_lo", "z_hi"]), axis=0)


def rope_tables(segments):
    slot_ids = jnp.arange(segments.shape[0], dtype=jnp.int32)
    seg_start = jnp.sum((segments[None, :] < segments[:, None]).astype(jnp.int32), axis=1)
    position = (slot_ids - seg_start).astype(F32)
    frequency = ROPE_THETA ** (-jnp.arange(0, HEAD, 2).astype(F32) / HEAD)
    angles = position[:, None] * frequency[None, :]
    cosine, sine = jnp.cos(angles), jnp.sin(angles)
    return (
        jnp.concatenate([cosine, cosine], axis=1),
        jnp.concatenate([sine, -sine], axis=1),
    )


def local(
    activations,
    queries,
    rotated_key_value,
    attention_out_grad,
    adapter_down,
    adapter_up,
    bin_local_index,
    bin_row_offset,
    spill_node,
    spill_row_offset,
    arrival_pick_index,
    packed_sequence_number,
):
    plan = (bin_local_index, bin_row_offset, spill_node, spill_row_offset)
    rows = (queries, attention_out_grad, rotated_key_value, activations)
    (near_send,) = pack(plan, *rows)
    far_send, far_x_send = pack(plan, *rows, adapter_down)

    near = lax.all_to_all(near_send, "local", split_axis=0, concat_axis=0, tiled=True)
    far_send, near = lax.optimization_barrier((far_send, near))
    far = lax.all_to_all(far_send, "node", split_axis=0, concat_axis=0, tiled=True)
    near_x, near_down = near_adapter_rows(near[:, :, ATT_COLS:], activations, adapter_down)
    pick_row = arrival_pick_index
    seg_row = packed_sequence_number
    cos, sin = rope_tables(packed_sequence_number.reshape(-1))
    far_x_send, far, near_x, near_down, cos, sin = lax.optimization_barrier(
        (far_x_send, far, near_x, near_down, cos, sin)
    )
    far_x = lax.all_to_all(far_x_send, "node", split_axis=0, concat_axis=0, tiled=True)

    kv_grad, lift = attention(
        pick_row,
        seg_row,
        cos,
        sin,
        adapter_up,
        queries,
        attention_out_grad,
        rotated_key_value,
        near,
        far,
    )
    keep, give, kv_grad = adapters(
        pick_row, near_down, activations, far_x, lift, near_x, kv_grad
    )
    total = sum_over_devices(keep, give) * (1.0 / math.sqrt(256 * ROWS))
    return (kv_grad, total[:DOWN_SHARD], total[DOWN_SHARD:])


def solution(mesh):
    split = P(("node", "local"), None)
    return jax.shard_map(
        local,
        mesh=mesh,
        in_specs=(split,) * 4 + (P(), P()) + (split,) * 6,
        out_specs=(split,) * 3,
        check_vma=False,
    )
```

```python
import functools
import math

import numpy as np

import jax
import jax.numpy as jnp
from jax import lax
from jax.experimental import pallas as pl
from jax.experimental.pallas import tpu as pltpu
from jax.sharding import PartitionSpec as P

KV_HEADS = 8
HEAD = 128
ADAPTER_RANK = 64
CAP_L = 4
CAP_N = 4
GROUP = 5
KEY_HEAD_WIDTH = 1024
MODEL_WIDTH = 5120
ROWS = 256
PEERS = 16
MOVED = PEERS * CAP_L
ARRIVALS = ROWS + 2 * MOVED
ROPE_THETA = 1000000.0

QUARTERS = 4
GROUP_WIDTH = GROUP * HEAD
HEAD_COLS = 2 * GROUP_WIDTH + 2 * HEAD
HEAD_QUARTER = HEAD_COLS // QUARTERS
ATT_COLS = KV_HEADS * HEAD_QUARTER
X_QUARTER = MODEL_WIDTH // QUARTERS
LOG2E = math.log2(math.e)
BF = jnp.bfloat16
F32 = jnp.float32
MIB = 1 << 20
VMEM_LIMIT = 62 * MIB

DOWN_SHARD = 20
UP_SHARD = 4
SHARD = DOWN_SHARD + UP_SHARD
BLOCK_DEV = 32
BLOCK_COUNT = 8
DOWN_BLOCK = BLOCK_DEV * DOWN_SHARD
UP_BLOCK = BLOCK_DEV * UP_SHARD
PARTS = 4
PART_ROWS = 4 * SHARD
PART_COLS = 3 * HEAD
PART_SHIFT = 32


def dot(a, b):
    return jnp.dot(a, b, preferred_element_type=F32)


def dot_nt(a, b):
    return lax.dot_general(a, b, (((1,), (1,)), ((), ())), preferred_element_type=F32)


def dot_tn(a, b):
    return lax.dot_general(a, b, (((0,), (0,)), ((), ())), preferred_element_type=F32)


def iota(shape, dim):
    return lax.broadcasted_iota(jnp.int32, shape, dim)


def interleave(rows, scratch):
    blocks = scratch.shape[0]
    for c in range(QUARTERS):
        for i in range(blocks):
            at = (c * blocks + i) * HEAD
            scratch[i, pl.ds(c, MOVED, stride=QUARTERS), :] = rows[:, at : at + HEAD]
    wide = jnp.concatenate([scratch[i] for i in range(blocks)], axis=1)
    return wide.astype(BF).reshape(PEERS, 16, blocks * HEAD)


def gather_quarters(rows, scratch):
    blocks = scratch.shape[0]
    wide = rows.reshape(ROWS, blocks * HEAD).astype(F32)
    for i in range(blocks):
        scratch[i] = wide[:, i * HEAD : (i + 1) * HEAD]
    return jnp.concatenate(
        [
            scratch[i, pl.ds(c, MOVED, stride=QUARTERS), :]
            for c in range(QUARTERS)
            for i in range(blocks)
        ],
        axis=1,
    ).astype(BF)


X_STEPS = 5
X_STEP = X_QUARTER // X_STEPS


def columns(j, width):
    return slice(j * width, (j + 1) * width)


def pack_kernel(near, bin_local, bin_offset, spill_node, spill_offset, q, g, kv, x, *rest):
    if near:
        att_out, *rest = rest
        x_out, x_from = att_out, ATT_COLS
    else:
        down, att_out, x_out, *rest = rest
        x_from = 0
    q_in, g_in, kv_in, x_in, att, att_x, spread, spread_x, head_sem, x_sem, out_sem, *rest = rest

    loads = [pltpu.make_async_copy(kv, kv_in, head_sem.at[2 * KV_HEADS])]
    for j in range(KV_HEADS):
        part = columns(j, GROUP_WIDTH)
        loads.append(pltpu.make_async_copy(q.at[:, part], q_in.at[:, part], head_sem.at[2 * j]))
        loads.append(
            pltpu.make_async_copy(g.at[:, part], g_in.at[:, part], head_sem.at[2 * j + 1])
        )
    x_loads = []
    for c in range(QUARTERS):
        part = columns(c, X_QUARTER)
        x_loads.append(pltpu.make_async_copy(x.at[:, part], x_in.at[:, part], x_sem.at[c]))
    if not near:
        down_in, att_down, down_sem = rest
        x_loads.append(pltpu.make_async_copy(down, down_in, down_sem.at[0]))
    middle = 1 + KV_HEADS
    for load in loads[:middle] + x_loads + loads[middle:]:
        load.start()

    stays_in = bin_local[...] == lax.axis_index("local")
    if near:
        target = jnp.where(stays_in, -1, bin_local[...] * CAP_L + bin_offset[...])
    else:
        moves = stays_in & (spill_node[...] != lax.axis_index("node"))
        target = jnp.where(moves, spill_node[...] * CAP_N + spill_offset[...], -1)
    select = jnp.where(iota((MOVED, ROWS), 0) == target, 1.0, 0.0).astype(BF)
    stores = []

    def send(source, to, sem):
        stores.append(pltpu.make_async_copy(source, to, sem))
        stores[-1].start()

    def pack_head(j):
        loads[1 + 2 * j].wait()
        loads[2 + 2 * j].wait()
        part = columns(j, GROUP_WIDTH)
        rows = jnp.concatenate(
            [
                q_in[:, part],
                g_in[:, part],
                kv_in[:, columns(j, HEAD)],
                kv_in[:, columns(KV_HEADS + j, HEAD)],
            ],
            axis=1,
        )
        part = columns(j, HEAD_QUARTER)
        att[:, :, part] = interleave(dot(select, rows), spread.at[j % 2])
        send(att.at[:, :, part], att_out.at[:, :, part], out_sem.at[j])

    loads[0].wait()
    for j in range(KV_HEADS // 2):
        pack_head(j)
    for load in x_loads:
        load.wait()
    moved_down = 0.0
    for j in range(X_STEPS):
        rows = jnp.concatenate(
            [x_in[:, columns(c * X_STEPS + j, X_STEP)] for c in range(QUARTERS)], axis=1
        )
        part = columns(j, X_STEP)
        picked = dot(select, rows)
        att_x[:, :, part] = interleave(picked, spread_x.at[j % 2])
        if not near:
            down_rows = jnp.concatenate(
                [down_in[columns(c * X_STEPS + j, X_STEP)] for c in range(QUARTERS)], axis=0
            )
            moved_down = moved_down + dot(picked.astype(BF), down_rows)
        to = slice(x_from + part.start, x_from + part.stop)
        send(att_x.at[:, :, part], x_out.at[:, :, to], out_sem.at[KV_HEADS + j])
    for j in range(KV_HEADS // 2, KV_HEADS):
        pack_head(j)
    if not near:
        picked = moved_down.astype(BF).astype(F32)
        rows = jnp.concatenate([picked] + [jnp.zeros_like(picked)] * (QUARTERS - 1), axis=1)
        att_down[...] = interleave(rows, spread_x.at[0, :1])
        send(att_down, x_out.at[:, :, X_QUARTER:], down_sem.at[1])
    for store in stores:
        store.wait()


def pack(plan, queries, grads, kv, activations, down=None):
    near = down is None
    hbm, vmem = pl.BlockSpec(memory_space=pltpu.HBM), pl.BlockSpec(memory_space=pltpu.VMEM)
    scratch = [
        pltpu.VMEM((ROWS, KV_HEADS * GROUP_WIDTH), BF),
        pltpu.VMEM((ROWS, KV_HEADS * GROUP_WIDTH), BF),
        pltpu.VMEM((ROWS, 2 * KEY_HEAD_WIDTH), BF),
        pltpu.VMEM((ROWS, MODEL_WIDTH), BF),
        pltpu.VMEM((PEERS, 16, ATT_COLS), BF),
        pltpu.VMEM((PEERS, 16, X_QUARTER), BF),
        pltpu.VMEM((2, HEAD_QUARTER // HEAD, ROWS, HEAD), F32),
        pltpu.VMEM((2, X_STEP // HEAD, ROWS, HEAD), F32),
        pltpu.SemaphoreType.DMA((2 * KV_HEADS + 1,)),
        pltpu.SemaphoreType.DMA((QUARTERS,)),
        pltpu.SemaphoreType.DMA((KV_HEADS + X_STEPS,)),
    ]
    if near:
        args, out_specs = (), [hbm]
        out_shape = [jax.ShapeDtypeStruct((PEERS, 16, ATT_COLS + X_QUARTER), BF)]
    else:
        args, out_specs = (down,), [hbm, hbm]
        out_shape = [
            jax.ShapeDtypeStruct((PEERS, 16, ATT_COLS), BF),
            jax.ShapeDtypeStruct((PEERS, 16, X_QUARTER + HEAD), BF),
        ]
        scratch += [
            pltpu.VMEM((MODEL_WIDTH, HEAD), BF),
            pltpu.VMEM((PEERS, 16, HEAD), BF),
            pltpu.SemaphoreType.DMA((2,)),
        ]
    return pl.pallas_call(
        functools.partial(pack_kernel, near),
        in_specs=[vmem] * 4 + [hbm] * (4 + len(args)),
        out_specs=out_specs,
        out_shape=out_shape,
        scratch_shapes=scratch,
        compiler_params=pltpu.CompilerParams(vmem_limit_bytes=VMEM_LIMIT),
        cost_estimate=pl.CostEstimate(
            flops=2 * MOVED * ROWS * QUARTERS * (ATT_COLS + X_QUARTER),
            bytes_accessed=14 * MIB,
            transcendentals=0,
        ),
        name="pack_rows",
    )(*plan, queries, grads, kv, activations, *args)


def near_kernel(near, x, down, near_x_out, down_out, spread):
    rows = gather_quarters(near[...], spread)
    near_x_out[...] = rows
    down_out[:ROWS] = dot(x[...], down[...]).astype(BF)
    down_out[ROWS:] = dot(rows, down[...]).astype(BF)


def near_adapter_rows(near, x, down):
    def whole(*shape):
        return pl.BlockSpec(shape, lambda i: (0,) * len(shape))

    return pl.pallas_call(
        near_kernel,
        grid=(1,),
        in_specs=[
            whole(PEERS, 16, X_QUARTER),
            whole(ROWS, MODEL_WIDTH),
            whole(MODEL_WIDTH, HEAD),
        ],
        out_specs=[whole(MOVED, MODEL_WIDTH), whole(ROWS + MOVED, HEAD)],
        out_shape=[
            jax.ShapeDtypeStruct((MOVED, 40 * MODEL_WIDTH), BF),
            jax.ShapeDtypeStruct((ROWS + MOVED, HEAD), BF),
        ],
        scratch_shapes=[pltpu.VMEM((X_QUARTER // HEAD, ROWS, HEAD), F32)],
        compiler_params=pltpu.CompilerParams(vmem_limit_bytes=32 * MIB),
        cost_estimate=pl.CostEstimate(
            flops=2 * MOVED * MODEL_WIDTH * HEAD, bytes_accessed=9 * MIB, transcendentals=0
        ),
        name="near_adapter_rows",
    )(near, x, down)


def to_column(row):
    diagonal = iota((ROWS, ROWS), 0) == iota((ROWS, ROWS), 1)
    return jnp.sum(jnp.where(diagonal, row, 0), axis=1, keepdims=True)


def arrival_pick(pick, entry):
    return jnp.where(pick == entry, 1.0, 0.0).astype(BF)


STEP_HEADS = 2


def head_grads(
    step, i, up, q, g, k, v, near, far, grad_out, gather, bias, lift, spread, spread_far, cos, sin
):
    part, wide = columns(i, HEAD), columns(i, GROUP_WIDTH)
    own_rows = jnp.concatenate([q[:, wide], g[:, wide], k[:, part], v[:, part]], axis=1)
    near_rows = gather_quarters(near[:, :, columns(i, HEAD_QUARTER)], spread.at[i])
    far_rows = gather_quarters(far[:, :, columns(i, HEAD_QUARTER)], spread_far.at[i])
    packed = dot(gather[...], jnp.concatenate([own_rows, near_rows, far_rows], axis=0)).astype(BF)
    key = packed[:, 2 * GROUP_WIDTH : 2 * GROUP_WIDTH + HEAD]
    value = packed[:, 2 * GROUP_WIDTH + HEAD :]
    score_scale = 1.0 / math.sqrt(HEAD)

    half = ROWS // 2
    sums = []
    for block in range(2):
        rows = slice(block * half, (block + 1) * half)
        keys = (block + 1) * half
        query = jnp.concatenate(
            [packed[rows, h * HEAD : (h + 1) * HEAD] for h in range(GROUP)], axis=0
        )
        grad = jnp.concatenate(
            [packed[rows, GROUP_WIDTH + h * HEAD : GROUP_WIDTH + (h + 1) * HEAD] for h in range(GROUP)],
            axis=0,
        )
        block_bias = jnp.concatenate([bias[:keys, rows]] * GROUP, axis=1)
        scores = dot_nt(key[:keys], query) * (score_scale * LOG2E) + block_bias
        weights = jnp.exp2(scores - jnp.max(scores, axis=0, keepdims=True))
        probs = weights * (1.0 / jnp.sum(weights, axis=0, keepdims=True))
        prob_grad = dot_nt(value[:keys], grad)
        delta = jnp.sum(probs * prob_grad, axis=0, keepdims=True)
        score_grad = (probs * (prob_grad - delta)).astype(BF)
        sums.append((dot(score_grad, query), dot(probs.astype(BF), grad)))
    key_rot = jnp.concatenate([sums[0][0] + sums[1][0][:half], sums[1][0][half:]], axis=0)
    value_grad = jnp.concatenate([sums[0][1] + sums[1][1][:half], sums[1][1][half:]], axis=0)
    key_rot = key_rot * score_scale
    swapped = jnp.concatenate([key_rot[:, HEAD // 2 :], key_rot[:, : HEAD // 2]], axis=1)
    key_grad = key_rot * cos[...] + swapped * sin[...]

    key_grad = key_grad.astype(BF)
    value_grad = value_grad.astype(BF)
    grad_out[:, pl.ds(pl.multiple_of((step * STEP_HEADS + i) * HEAD, HEAD), HEAD)] = key_grad
    grad_out[:, pl.ds(
        pl.multiple_of(KEY_HEAD_WIDTH + (step * STEP_HEADS + i) * HEAD, HEAD), HEAD
    )] = value_grad
    up_rows = up[:, part]
    zero = jnp.zeros((ADAPTER_RANK, HEAD), BF)
    key_up = jnp.concatenate([up_rows[:ADAPTER_RANK], zero], axis=0)
    value_up = jnp.concatenate([zero, up_rows[ADAPTER_RANK:]], axis=0)
    lift[...] += dot_nt(
        jnp.concatenate([key_grad, value_grad], axis=1),
        jnp.concatenate([key_up, value_up], axis=1),
    )


def attention_kernel(
    pick_row, seg_row, cos, sin, up, q, g, k, v, near, far, grad_out, lift_out,
    gather, bias, lift, spread, spread_far
):
    step = pl.program_id(0)

    @pl.when(step == 0)
    def _():
        gather[...] = arrival_pick(to_column(pick_row[...]), iota((ROWS, ARRIVALS), 1))
        allowed = (to_column(seg_row[...]) == seg_row[...]) & (
            iota((ROWS, ROWS), 0) <= iota((ROWS, ROWS), 1)
        )
        bias[...] = jnp.where(allowed, 0.0, -1e30)
        lift[...] = jnp.zeros_like(lift)

    for i in range(STEP_HEADS):
        head_grads(step, i, up, q, g, k, v, near, far, grad_out, gather, bias, lift, spread, spread_far, cos, sin)

    @pl.when(step == KV_HEADS // STEP_HEADS - 1)
    def _():
        lift_out[...] = lift[...].astype(BF)


def attention(pick_row, seg_row, cos, sin, up, queries, grads, kv, near, far):
    def whole(shape):
        return pl.BlockSpec(shape, lambda j: (0,) * len(shape))

    def head_block(width):
        return pl.BlockSpec((ROWS, width), lambda j: (0, j))

    arrived = pl.BlockSpec((PEERS, 16, STEP_HEADS * HEAD_QUARTER), lambda j: (0, 0, j))
    return pl.pallas_call(
        attention_kernel,
        grid=(KV_HEADS // STEP_HEADS,),
        in_specs=[
            whole((1, ROWS)),
            whole((1, ROWS)),
            whole((ROWS, HEAD)),
            whole((ROWS, HEAD)),
            pl.BlockSpec((2 * ADAPTER_RANK, STEP_HEADS * HEAD), lambda j: (0, j)),
            head_block(STEP_HEADS * GROUP_WIDTH),
            head_block(STEP_HEADS * GROUP_WIDTH),
            head_block(STEP_HEADS * HEAD),
            pl.BlockSpec((ROWS, STEP_HEADS * HEAD), lambda j: (0, KV_HEADS // STEP_HEADS + j)),
            arrived,
            arrived,
        ],
        out_specs=[whole((ROWS, 2 * KEY_HEAD_WIDTH)), whole((ROWS, HEAD))],
        out_shape=[
            jax.ShapeDtypeStruct((ROWS, 2 * KEY_HEAD_WIDTH), BF),
            jax.ShapeDtypeStruct((ROWS, 384 * HEAD), BF),
        ],
        scratch_shapes=[
            pltpu.VMEM((ROWS, ARRIVALS), BF),
            pltpu.VMEM((ROWS, ROWS), F32),
            pltpu.VMEM((ROWS, HEAD), F32),
            pltpu.VMEM((STEP_HEADS, HEAD_QUARTER // HEAD, ROWS, HEAD), F32),
            pltpu.VMEM((STEP_HEADS, HEAD_QUARTER // HEAD, ROWS, HEAD), F32),
        ],
        compiler_params=pltpu.CompilerParams(vmem_limit_bytes=54 * MIB),
        cost_estimate=pl.CostEstimate(
            flops=12 * 10**9, bytes_accessed=14 * MIB, transcendentals=2 * 10**6
        ),
        name="attention_grads",
    )(pick_row, seg_row, cos, sin, up, queries, grads, kv, kv, near, far)


def adapter_kernel(
    pick_row, first_core, core_step, near_down, x, far, lift, near_x, kv_grad,
    keep, give, _kv_grad, lift_in, near_in, kv_in, far_in, placed_out, spread, load_sem, out_sem
):
    loads = [
        pltpu.make_async_copy(source, to, load_sem.at[i])
        for i, (source, to) in enumerate(
            (
                (lift.at[:, :HEAD], lift_in),
                (far, far_in),
                (kv_grad, kv_in),
                (near_x.at[:, :MODEL_WIDTH], near_in),
            )
        )
    ]
    for load in loads:
        load.start()

    core = lax.rem(lax.axis_index("local"), 2)
    column = iota((PART_ROWS, PART_COLS), 1)
    orders = [
        jnp.concatenate(
            [
                jnp.where(
                    column == first_core[...] + (at * core_step[...] + k * PART_SHIFT), 1.0, 0.0
                ).astype(BF)
                for at in (core, 1 - core)
            ],
            axis=0,
        )
        for k in range(PARTS)
    ]
    gather = arrival_pick(to_column(pick_row[...]), iota((ROWS, ARRIVALS), 1))
    spread_lift = arrival_pick(pick_row[...], iota((ARRIVALS, ROWS), 0))
    loads[0].wait()
    lifted = dot(spread_lift, lift_in[...]).astype(BF)

    loads[1].wait()
    far_rows = gather_quarters(far_in[:, :, :X_QUARTER], spread)
    spread[0] = far_in[:, :, X_QUARTER:].reshape(ROWS, HEAD).astype(F32)
    far_down = spread[0, pl.ds(0, MOVED, stride=QUARTERS), :].astype(BF)

    arrived_down = jnp.concatenate([near_down[...], far_down], axis=0)
    down_out = dot(gather, arrived_down).astype(BF)
    loads[2].wait()
    up_both = dot_tn(down_out, kv_in[...])
    up_sum = jnp.concatenate(
        [up_both[:ADAPTER_RANK, :KEY_HEAD_WIDTH], up_both[ADAPTER_RANK:, KEY_HEAD_WIDTH:]], axis=0
    ).astype(BF)

    loads[3].wait()
    stores = []
    for z_lo in range(BLOCK_COUNT // 2):
        part = columns(z_lo, X_QUARTER)
        arrived = jnp.concatenate([x[:, part], near_in[:, part], far_rows[:, part]], axis=0)
        down_sum = dot_tn(lifted, arrived).astype(BF)
        rows = columns(z_lo, 2 * SHARD)
        for k in range(PARTS):
            y_low, x_high = k // 2, k % 2
            both = []
            for y_high in range(2):
                start = y_high * DOWN_BLOCK + k * HEAD
                both.append(
                    jnp.concatenate(
                        [
                            down_sum[:, start : start + 2 * HEAD],
                            up_sum[:, columns(2 * z_lo + y_high, UP_BLOCK)],
                        ],
                        axis=1,
                    )
                )
            placed = dot_nt(orders[k], jnp.concatenate(both, axis=0)).astype(BF)
            for c in range(2):
                for x_low in range(2):
                    at = (c * 2 + x_low) * 2 * SHARD
                    for y_high in range(2):
                        y = y_high * 2 + y_low
                        placed_out[c, (x_high * 2 + x_low) * 4 + y, rows, :] = placed[
                            at : at + 2 * SHARD, columns(y_high, HEAD)
                        ]
        for c, out in enumerate((give, keep)):
            stores.append(
                pltpu.make_async_copy(
                    placed_out.at[1 - c, :, rows], out.at[:, rows], out_sem.at[2 * z_lo + c]
                )
            )
            stores[-1].start()
    for store in stores:
        store.wait()


def shard_order():
    order, step = [], []
    for x_low in range(2):
        for z_hi in range(2):
            device = (x_low * 2 + z_hi) * 2
            order += [device * DOWN_SHARD + r for r in range(DOWN_SHARD)]
            order += [2 * HEAD + device * UP_SHARD + r for r in range(UP_SHARD)]
            step += [DOWN_SHARD] * DOWN_SHARD + [UP_SHARD] * UP_SHARD
    return [np.asarray(a, np.int32).reshape(PART_ROWS, 1) for a in (order, step)]


def adapters(pick_row, near_down, x, far, lift, near_x, kv_grad):
    hbm, vmem = pl.BlockSpec(memory_space=pltpu.HBM), pl.BlockSpec(memory_space=pltpu.VMEM)
    place = pl.BlockSpec(memory_space=pl.ANY)
    first_core, core_step = [jnp.asarray(a) for a in shard_order()]
    half = jax.ShapeDtypeStruct((16, 8 * SHARD, HEAD), BF)
    passed = jax.ShapeDtypeStruct(kv_grad.shape, kv_grad.dtype)
    return pl.pallas_call(
        adapter_kernel,
        out_shape=[half, half, passed],
        input_output_aliases={8: 2},
        in_specs=[vmem] * 5 + [hbm] * 4,
        out_specs=[place, place, hbm],
        scratch_shapes=[
            pltpu.VMEM((ROWS, HEAD), BF),
            pltpu.VMEM((MOVED, MODEL_WIDTH), BF),
            pltpu.VMEM((ROWS, 2 * KEY_HEAD_WIDTH), BF),
            pltpu.VMEM((PEERS, 16, X_QUARTER + HEAD), BF),
            pltpu.VMEM((2, 16, 8 * SHARD, HEAD), BF),
            pltpu.VMEM((X_QUARTER // HEAD, ROWS, HEAD), F32),
            pltpu.SemaphoreType.DMA((4,)),
            pltpu.SemaphoreType.DMA((BLOCK_COUNT,)),
        ],
        compiler_params=pltpu.CompilerParams(vmem_limit_bytes=40 * MIB),
        cost_estimate=pl.CostEstimate(
            flops=4 * 10**9, bytes_accessed=10 * MIB, transcendentals=0
        ),
        name="adapter_grads",
    )(pick_row, first_core, core_step, near_down, x, far, lift, near_x, kv_grad)


def device_groups(axes):
    names = ["z_lo", "y", "x", "z_hi", "core"]
    index = np.arange(256).reshape(4, 4, 4, 2, 2)
    moved = [names.index(a) for a in axes]
    rest = [i for i in range(5) if i not in moved]
    size = math.prod(index.shape[i] for i in moved)
    return index.transpose(rest + moved).reshape(-1, size).tolist()


def exchange(array, axes):
    return lax.all_to_all(
        array,
        ("node", "local"),
        split_axis=0,
        concat_axis=0,
        axis_index_groups=device_groups(axes),
        tiled=True,
    )


def sum_over_devices(keep, give):
    got = lax.ppermute(give, ("node", "local"), [(i, i ^ 1) for i in range(256)])
    total = (keep.astype(F32) + got.astype(F32)).astype(BF)
    total = jnp.sum(exchange(total, ["x", "y"]).astype(F32), axis=0)
    total = total.reshape(8, SHARD, HEAD)
    return jnp.sum(exchange(total, ["z_lo", "z_hi"]), axis=0)


def rope_tables(segments):
    slot_ids = jnp.arange(segments.shape[0], dtype=jnp.int32)
    seg_start = jnp.sum((segments[None, :] < segments[:, None]).astype(jnp.int32), axis=1)
    position = (slot_ids - seg_start).astype(F32)
    frequency = ROPE_THETA ** (-jnp.arange(0, HEAD, 2).astype(F32) / HEAD)
    angles = position[:, None] * frequency[None, :]
    cosine, sine = jnp.cos(angles), jnp.sin(angles)
    return (
        jnp.concatenate([cosine, cosine], axis=1),
        jnp.concatenate([sine, -sine], axis=1),
    )


def local(
    activations,
    queries,
    rotated_key_value,
    attention_out_grad,
    adapter_down,
    adapter_up,
    bin_local_index,
    bin_row_offset,
    spill_node,
    spill_row_offset,
    arrival_pick_index,
    packed_sequence_number,
):
    plan = (bin_local_index, bin_row_offset, spill_node, spill_row_offset)
    rows = (queries, attention_out_grad, rotated_key_value, activations)
    (near_send,) = pack(plan, *rows)
    far_send, far_x_send = pack(plan, *rows, adapter_down)

    near = lax.all_to_all(near_send, "local", split_axis=0, concat_axis=0, tiled=True)
    far_send, near = lax.optimization_barrier((far_send, near))
    far = lax.all_to_all(far_send, "node", split_axis=0, concat_axis=0, tiled=True)
    near_x, near_down = near_adapter_rows(near[:, :, ATT_COLS:], activations, adapter_down)
    pick_row = arrival_pick_index
    seg_row = packed_sequence_number
    cos, sin = rope_tables(packed_sequence_number.reshape(-1))
    far_x_send, far, near_x, near_down, cos, sin = lax.optimization_barrier(
        (far_x_send, far, near_x, near_down, cos, sin)
    )
    far_x = lax.all_to_all(far_x_send, "node", split_axis=0, concat_axis=0, tiled=True)

    kv_grad, lift = attention(
        pick_row,
        seg_row,
        cos,
        sin,
        adapter_up,
        queries,
        attention_out_grad,
        rotated_key_value,
        near,
        far,
    )
    keep, give, kv_grad = adapters(
        pick_row, near_down, activations, far_x, lift, near_x, kv_grad
    )
    total = sum_over_devices(keep, give) * (1.0 / math.sqrt(256 * ROWS))
    return (kv_grad, total[:DOWN_SHARD], total[DOWN_SHARD:])


def solution(mesh):
    split = P(("node", "local"), None)
    return jax.shard_map(
        local,
        mesh=mesh,
        in_specs=(split,) * 4 + (P(), P()) + (split,) * 6,
        out_specs=(split,) * 3,
        check_vma=False,
    )
```
